512 devices in a mesh: ctx: 64 (over y, z), head: 8 (over x, core).
Axes of the slice: x: 4, y: 8, z: 8, core: 2. Of those that a mesh axis runs over, the one named last changes fastest.
Arguments:
- queries: bfloat16 [8192, 2048], P('ctx', 'head'), may hold values from -6 to 6
- key_rows: bfloat16 [8192, 2048], P('ctx', 'head'), may hold values from -6 to 6
- value_rows: bfloat16 [8192, 4096], P('ctx', 'head'), may hold values from -6 to 6
- beta_logit: float32 [8192, 32], P('ctx', 'head'), may hold values from -7 to 2
- log_decay: float32 [8192, 32], P('ctx', 'head'), may hold values from -1 to 0
- out_gate: bfloat16 [8192, 4096], P('ctx', 'head'), may hold values from -6 to 6
- norm_gain: float32 [128], replicated, may hold values from 0.25 to 1.75
- out_weight: bfloat16 [4096, 2048], P('head'), may hold values from -0.09375 to 0.09375
Outputs:
- mixed: bfloat16 [8192, 2048], P('ctx', 'head')
The draws below stay inside these ranges and needn't reach their ends.
All inputs are finite; a program needn't handle non-finite values.
Results may differ from the reference program's by a relative error of at most 0.005.
Values sent between devices are 32-bit elements; how exact they have to be, the bound alone decides.
A program may use at most 128 MiB of HBM per device.

```python
import math
import jax
import jax.numpy as jnp
from jax import lax

VALUE_HEADS = 32
KEY_HEADS = 16
HEAD_DIM = 128
MODEL_DIM = 2048
TOK_DEV = 128
LENGTH = 8192


def lasting_heads(key, share):
    return jax.random.uniform(key, (VALUE_HEADS,)) < share


def draw_beta_logit(key, part):
    share = 0.5
    lasting = lasting_heads(key, share)
    key = jax.random.fold_in(key, 11)
    keys = jax.random.split(key, 2)
    faint_logit = jax.random.uniform(keys[0], (LENGTH, VALUE_HEADS), minval=-7.0, maxval=-5.0)
    strong_logit = jax.random.uniform(keys[1], (LENGTH, VALUE_HEADS), minval=-2.0, maxval=2.0)
    return jnp.where(lasting[None, :], faint_logit, strong_logit).astype(jnp.float32)


def draw_log_decay(key, part):
    share = 0.5
    slow = lasting_heads(key, share)
    key = jax.random.fold_in(key, 7)
    keys = jax.random.split(key, 7)
    slow_rate = jnp.exp(jax.random.uniform(keys[1], (VALUE_HEADS,), minval=math.log(0.05), maxval=math.log(0.4))) / LENGTH
    fast_rate = jax.random.uniform(keys[2], (VALUE_HEADS,), minval=1.0 / 50.0, maxval=1.0 / 30.0)
    head_decay_rate = jnp.where(slow, slow_rate, fast_rate)
    coarse_estimate = jnp.exp(jax.random.uniform(keys[3], (LENGTH, VALUE_HEADS), minval=math.log(0.5), maxval=math.log(2.0)))
    split_multiplier = jnp.exp(jax.random.uniform(keys[4], (LENGTH // TOK_DEV, 1), minval=math.log(0.5), maxval=math.log(2.0)))
    split_multiplier = jnp.repeat(split_multiplier, TOK_DEV, axis=0)
    spots = jax.random.randint(keys[5], (3,), 0, LENGTH)
    error_value = jax.random.uniform(keys[6], (3, VALUE_HEADS), minval=0.2, maxval=0.5)
    erased_value = (jnp.arange(LENGTH)[:, None] == spots[None, :]).astype(jnp.float32)
    write_pulse = jnp.sum(erased_value[:, :, None] * (-jnp.log1p(-error_value))[None, :, :], axis=1)
    return (-(head_decay_rate[None, :] * coarse_estimate * split_multiplier) - write_pulse).astype(jnp.float32)


def levels(key, extent, shards, least, high):
    level = 1.0
    for axis_at, parts in shards:
        draws = jax.random.uniform(jax.random.fold_in(jax.random.fold_in(key, 6), axis_at), (parts,), jnp.float32, least / len(shards), high / len(shards))
        level = level * jnp.repeat(jnp.exp(draws), extent[axis_at] // parts).reshape((-1,) + (1,) * (len(extent) - 1 - axis_at))
    return level


def normal_values(own_key, shape, deviation, reach, shards=(), dtype=jnp.bfloat16):
    array = deviation * jax.random.normal(own_key, shape, jnp.float32)
    if shards:
        array = array * levels(own_key, shape, shards, -0.22, 0.18)
    return jnp.clip(array, -reach, reach).astype(dtype)


def setup_inputs(seed: int = 0) -> dict:
    key_list = jax.random.split(jax.random.key(seed), 9)
    return {
        "queries": normal_values(key_list[0], (LENGTH, KEY_HEADS * HEAD_DIM), 1.0, 6.0, ((0, 64), (1, 8))),
        "key_rows": normal_values(key_list[1], (LENGTH, KEY_HEADS * HEAD_DIM), 1.0, 6.0, ((0, 64), (1, 8))),
        "value_rows": normal_values(key_list[2], (LENGTH, VALUE_HEADS * HEAD_DIM), 1.0, 6.0, ((0, 64), (1, 8))),
        "beta_logit": draw_beta_logit(jax.random.fold_in(key_list[8], 71), 0),
        "log_decay": draw_log_decay(jax.random.fold_in(key_list[8], 71), 0),
        "out_gate": normal_values(key_list[5], (LENGTH, VALUE_HEADS * HEAD_DIM), 1.0, 6.0, ((0, 64), (1, 8))),
        "norm_gain": jnp.clip(1.0 + 0.15 * jax.random.normal(key_list[6], (HEAD_DIM,), jnp.float32), 0.25, 1.75),
        "out_weight": normal_values(key_list[7], (VALUE_HEADS * HEAD_DIM, MODEL_DIM), (VALUE_HEADS * HEAD_DIM) ** -0.5, 0.09375, ((0, 8),)),
    }


def reference(queries, key_rows, value_rows, beta_logit, log_decay, out_gate, norm_gain, out_weight):
    top_precision = lax.Precision.HIGHEST
    group_size = VALUE_HEADS // KEY_HEADS
    query_head = queries.astype(jnp.float32).reshape(LENGTH, KEY_HEADS, HEAD_DIM)
    query_head = jnp.repeat(query_head, group_size, axis=1)
    key_head = key_rows.astype(jnp.float32).reshape(LENGTH, KEY_HEADS, HEAD_DIM)
    key_head = key_head * lax.rsqrt(lax.optimization_barrier(jnp.sum(key_head * key_head, axis=-1, keepdims=True)) + 1e-06)
    key_head = jnp.repeat(key_head, group_size, axis=1)
    value_head = value_rows.astype(jnp.float32).reshape(LENGTH, VALUE_HEADS, HEAD_DIM)
    beta_head = jax.nn.sigmoid(beta_logit.astype(jnp.float32))
    decay_head = jnp.exp(log_decay.astype(jnp.float32))

    def advance(present_state, pieces):
        query_at_step, key_at_step, value_t, beta_t, decay_t = pieces
        recalled_value = jnp.einsum('wj,wjn->wn', key_at_step, present_state, precision=top_precision)
        scaled = beta_t[:, None, None] * key_at_step[:, :, None]
        present_state = decay_t[:, None, None] * (present_state - scaled * recalled_value[:, None, :]) + scaled * value_t[:, None, :]
        return (present_state, jnp.einsum('wj,wjn->wn', query_at_step, present_state, precision=top_precision))
    start_state = jnp.zeros((VALUE_HEADS, HEAD_DIM, HEAD_DIM), jnp.float32)
    _, core_out = lax.scan(advance, start_state, (query_head, key_head, value_head, beta_head, decay_head), unroll=4)
    gate_head = out_gate.astype(jnp.float32).reshape(LENGTH, VALUE_HEADS, HEAD_DIM)
    normed = core_out * lax.rsqrt(lax.optimization_barrier(jnp.mean(core_out * core_out, axis=-1, keepdims=True)) + 1e-06)
    normed = normed * norm_gain * jax.nn.silu(gate_head)
    gated_out = normed.astype(jnp.bfloat16).reshape(LENGTH, VALUE_HEADS * HEAD_DIM)
    return jnp.dot(gated_out, out_weight, preferred_element_type=jnp.float32).astype(jnp.bfloat16)
```

```python
import functools

import jax
import jax.numpy as jnp
from jax import lax
from jax.experimental import pallas as pl
from jax.experimental.pallas import tpu as pltpu
from jax.sharding import PartitionSpec as P

MESH = pl.DeviceIdType.MESH
F32 = jnp.float32
BF16 = jnp.bfloat16
D = 128


def mm(a, b):
    batch = tuple(range(a.ndim - 2))
    dims = (((a.ndim - 1,), (b.ndim - 2,)), (batch, batch))
    return lax.dot_general(a, b, dims, precision=lax.Precision.HIGHEST, preferred_element_type=F32)


def mm_bf16(a, b):
    batch = tuple(range(a.ndim - 2))
    dims = (((a.ndim - 1,), (b.ndim - 2,)), (batch, batch))
    return lax.dot_general(a, b, dims, preferred_element_type=F32)


def mm_split(a, b):
    high = a.astype(BF16)
    low = (a - high.astype(F32)).astype(BF16)
    return mm_bf16(high, b) + mm_bf16(low, b)


def nt(a, b):
    return lax.dot_general(
        a, b, (((1,), (1,)), ((), ())), precision=lax.Precision.HIGHEST, preferred_element_type=F32
    )


def iotas(n):
    return (
        lax.broadcasted_iota(jnp.int32, (n, n), 0),
        lax.broadcasted_iota(jnp.int32, (n, n), 1),
    )


def unit_lower_inverse(strict_part):
    row, col = iotas(D)
    eye = jnp.where(row == col, 1.0, 0.0).astype(F32)

    def off(half):
        shift = half.bit_length() - 1
        rb, cb = row >> shift, col >> shift
        mask = ((rb ^ cb) == 1) & (rb > cb)
        return jnp.where(mask[None], strict_part, 0.0)

    inverse = eye[None] - off(1)
    half = 2
    while half < D:
        inverse = inverse - mm(inverse, mm(off(half), inverse))
        half *= 2
    return inverse


def after(later, earlier):
    both = mm(later[:, :D], earlier)
    return both + jnp.concatenate([jnp.zeros((D, D), F32), later[:, D:]], axis=1)


def ctx_kernel(
    ny,
    nz,
    q_ref,
    k_ref,
    v_ref,
    beta_ref,
    decay_ref,
    gate_ref,
    gain_ref,
    out_ref,
    own,
    zin,
    yin,
    tot_ref,
    prefix,
    sout,
    sin,
    within,
    qmap,
    state_ref,
    zsend,
    zrecv,
    ysend,
    yrecv,
    rsend,
    rrecv,
):
    heads = v_ref.shape[1] // D
    kheads = k_ref.shape[1] // D
    group = heads // kheads
    ctx, head = lax.axis_index("ctx"), lax.axis_index("head")
    y, z, core = ctx // nz, ctx % nz, head % 2
    barrier = pltpu.get_barrier_semaphore()
    for step in range(1, nz):
        pl.semaphore_signal(
            barrier, inc=1, device_id=(y * nz + (z + step) % nz, head), device_id_type=MESH
        )
    for step in range(1, ny):
        pl.semaphore_signal(
            barrier, inc=1, device_id=(((y + step) % ny) * nz + z, head), device_id_type=MESH
        )

    row, col = iotas(D)
    causal, strict = row >= col, row > col
    eye = jnp.where(row == col, 1.0, 0.0).astype(F32)
    tri = jnp.where(causal, 1.0, 0.0).astype(F32)
    keys = jnp.stack([k_ref[:, i * D : (i + 1) * D] for i in range(kheads)])
    queries = jnp.stack([q_ref[:, i * D : (i + 1) * D] for i in range(kheads)])
    values = jnp.stack([v_ref[:, i * D : (i + 1) * D] for i in range(heads)])
    keys32 = keys.astype(F32)
    keys_t32 = jnp.stack([keys32[i].T for i in range(kheads)])
    keys_t = keys_t32.astype(BF16)
    r_col = lax.rsqrt(jnp.sum(keys32 * keys32, axis=2, keepdims=True) + 1e-06)
    r_row = lax.rsqrt(jnp.sum(keys_t32 * keys_t32, axis=1, keepdims=True) + 1e-06)
    gram = mm_bf16(keys, keys_t) * (r_col * r_row)
    scores = mm_bf16(queries, keys_t) * r_row

    beta_row = jax.nn.sigmoid(beta_ref[...])
    decay_row = decay_ref[...]
    cum_row = nt(decay_row, tri)
    cum_col = nt(tri, decay_row)
    beta_col = nt(eye, beta_row)
    exp_row = jnp.exp(cum_row)
    exp_col = jnp.exp(cum_col)
    total = cum_row[:, D - 1 : D]
    exp_total = jnp.exp(total)
    tail_row = jnp.exp(total - cum_row)

    def per_head(fn):
        return jnp.stack([fn(h) for h in range(heads)])

    decay_mat = per_head(
        lambda h: jnp.exp(
            jnp.where(causal, cum_col[:, h : h + 1] - cum_row[h : h + 1, :], -1e30)
        )
    )
    strict_part = per_head(
        lambda h: jnp.where(
            strict, beta_col[:, h : h + 1] * gram[h // group] * decay_mat[h], 0.0
        )
    )
    inverse = unit_lower_inverse(strict_part)
    scaled = per_head(lambda h: inverse[h] * beta_row[h : h + 1, :])
    pseudo = mm_split(scaled, values)
    wy = mm_split(
        per_head(lambda h: scaled[h] * (exp_row[h : h + 1, :] * r_row[h // group])),
        per_head(lambda h: keys[h // group]),
    )
    wy_pseudo = jnp.concatenate([wy, pseudo], axis=2)
    tails = per_head(
        lambda h: keys_t32[h // group] * (r_row[h // group] * tail_row[h : h + 1, :])
    )
    block = mm(tails, wy_pseudo)
    for h in range(heads):
        own[h, :, :D] = exp_total[h : h + 1, :] * eye - block[h, :, :D]
        own[h, :, D:] = block[h, :, D:]

    pl.semaphore_wait(barrier, nz - 1 + ny - 1)

    def head_copy(h):
        return pltpu.make_async_remote_copy(
            src_ref=own.at[h],
            dst_ref=zin.at[z],
            send_sem=zsend.at[h],
            recv_sem=zrecv.at[z],
            device_id=(y * nz + 2 * h + core, head),
            device_id_type=MESH,
        )

    for h in range(heads):
        @pl.when(z != 2 * h + core)
        def _():
            head_copy(h).start()

        @pl.when(z == 2 * h + core)
        def _():
            zin[pl.ds(z, 1)] = own[h : h + 1]

    mixed = mm(per_head(lambda h: scores[h // group] * decay_mat[h]), wy_pseudo)
    for h in range(heads):
        within[h] = mixed[h, :, D:]
        qmap[h] = exp_col[:, h : h + 1] * queries[h // group].astype(F32) - mixed[h, :, :D]

    worker = (z % 2) == core

    def total_copy(target):
        return pltpu.make_async_remote_copy(
            src_ref=tot_ref,
            dst_ref=yin.at[y],
            send_sem=ysend.at[target],
            recv_sem=yrecv.at[y],
            device_id=(target * nz + z, head),
            device_id_type=MESH,
        )

    def state_copy(target):
        return pltpu.make_async_remote_copy(
            src_ref=sout.at[target],
            dst_ref=sin.at[z // 2],
            send_sem=rsend.at[target],
            recv_sem=rrecv.at[z // 2],
            device_id=(y * nz + target, head),
            device_id_type=MESH,
        )

    @pl.when(worker)
    def _():
        for i in range(nz):
            @pl.when(z != i)
            def _():
                pltpu.make_async_remote_copy(
                    src_ref=own.at[0],
                    dst_ref=zin.at[i],
                    send_sem=zsend.at[0],
                    recv_sem=zrecv.at[i],
                    device_id=(ctx, head),
                    device_id_type=MESH,
                ).wait_recv()

        level = {(i, i + 1): zin[i] for i in range(nz)}
        span = 1
        while span < nz:
            for i in range(0, nz, 2 * span):
                level[(i, i + 2 * span)] = after(
                    level[(i + span, i + 2 * span)], level[(i, i + span)]
                )
            span *= 2
        tot_ref[...] = level[(0, nz)]
        for target in range(1, ny):
            @pl.when(target > y)
            def _():
                total_copy(target).start()

        for i in range(1, nz):
            if (0, i) not in level:
                low = 1 << (i.bit_length() - 1)
                rest = i - low
                part = (low, i)
                if part not in level:
                    step = rest & -rest
                    level[part] = None
                    level[(0, i)] = after(level[(i - step, i)], level[(0, i - step)])
                else:
                    level[(0, i)] = after(level[part], level[(0, low)])
            prefix[i] = level[(0, i)]

        state_ref[...] = jnp.zeros((D, D), F32)
        for i in range(ny - 1):
            @pl.when(i < y)
            def _():
                pltpu.make_async_remote_copy(
                    src_ref=tot_ref,
                    dst_ref=yin.at[i],
                    send_sem=ysend.at[0],
                    recv_sem=yrecv.at[i],
                    device_id=(ctx, head),
                    device_id_type=MESH,
                ).wait_recv()
                state_ref[...] = mm(yin[i, :, :D], state_ref[...]) + yin[i, :, D:]

        state = state_ref[...]
        for i in range(nz):
            if i == 0:
                sout[i] = state
            else:
                sout[i] = mm(prefix[i, :, :D], state) + prefix[i, :, D:]

            @pl.when(z != i)
            def _():
                state_copy(i).start()

            @pl.when(z == i)
            def _():
                sin[pl.ds(z // 2, 1)] = sout[i : i + 1]

    for h in range(heads):
        @pl.when(z != 2 * h + core)
        def _():
            pltpu.make_async_remote_copy(
                src_ref=sout.at[0],
                dst_ref=sin.at[h],
                send_sem=rsend.at[0],
                recv_sem=rrecv.at[h],
                device_id=(ctx, head),
                device_id_type=MESH,
            ).wait_recv()

    core_out = within[...] + mm(qmap[...], sin[...])
    normed = core_out * lax.rsqrt(jnp.mean(core_out * core_out, axis=2, keepdims=True) + 1e-06)
    for h in range(heads):
        gate = gate_ref[:, h * D : (h + 1) * D].astype(F32)
        out_ref[:, h * D : (h + 1) * D] = (
            normed[h] * gain_ref[...] * (gate / (1.0 + jnp.exp(-gate)))
        ).astype(BF16)

    for h in range(heads):
        @pl.when(z != 2 * h + core)
        def _():
            head_copy(h).wait_send()

    @pl.when(worker)
    def _():
        for target in range(1, ny):
            @pl.when(target > y)
            def _():
                total_copy(target).wait_send()
        for i in range(nz):
            @pl.when(z != i)
            def _():
                state_copy(i).wait_send()


def head_kernel(
    n, gated_ref, weight_ref, out_ref, pair_out, pair_in, mine, chip_in, psend, precv, csend, crecv
):
    chips = n // 2
    width = out_ref.shape[1]
    ctx, head = lax.axis_index("ctx"), lax.axis_index("head")
    x, core = head // 2, head % 2
    sibling = x * 2 + 1 - core
    barrier = pltpu.get_barrier_semaphore()
    pl.semaphore_signal(barrier, inc=1, device_id=(ctx, sibling), device_id_type=MESH)
    for step in range(1, chips):
        pl.semaphore_signal(
            barrier,
            inc=1,
            device_id=(ctx, ((x + step) % chips) * 2 + core),
            device_id_type=MESH,
        )
    gated = gated_ref[...]

    def columns(chip, which):
        start = pl.multiple_of((chip * 2 + which) * width, width)
        return mm_bf16(gated, weight_ref[:, pl.ds(start, width)])

    def pair_copy(step):
        return pltpu.make_async_remote_copy(
            src_ref=pair_out.at[step],
            dst_ref=pair_in.at[step],
            send_sem=psend.at[step],
            recv_sem=precv.at[step],
            device_id=(ctx, sibling),
            device_id_type=MESH,
        )

    def chip_copy(step):
        return pltpu.make_async_remote_copy(
            src_ref=mine.at[step],
            dst_ref=chip_in.at[step],
            send_sem=csend.at[step],
            recv_sem=crecv.at[step],
            device_id=(ctx, ((x + step) % chips) * 2 + core),
            device_id_type=MESH,
        )

    order = sorted(range(chips), key=lambda s: -min(s, chips - s))
    for step in order:
        pair_out[step] = columns((x + step) % chips, 1 - core)
    pl.semaphore_wait(barrier, chips)
    for step in order:
        pair_copy(step).start()
    for step in order:
        mine[step] = columns((x + step) % chips, core)
    for step in order:
        pair_copy(step).wait_recv()
        mine[step] = mine[step] + pair_in[step]
        if step:
            chip_copy(step).start()
    total = mine[0]
    for step in order[1:-1] + order[:-1][:1]:
        chip_copy(step).wait_recv()
        total = total + chip_in[step]
    out_ref[...] = total.astype(BF16)
    for step in order:
        pair_copy(step).wait_send()
        if step:
            chip_copy(step).wait_send()


def per_device(
    queries, key_rows, value_rows, beta_logit, log_decay, out_gate, norm_gain, out_weight
):
    heads = value_rows.shape[1] // D
    tokens = value_rows.shape[0]
    nz = 2 * heads
    ny = lax.axis_size("ctx") // nz
    n = lax.axis_size("head")
    width = out_weight.shape[1] // n
    vmem = pl.BlockSpec(memory_space=pltpu.VMEM)
    dma = pltpu.SemaphoreType.DMA
    gated = pl.pallas_call(
        functools.partial(ctx_kernel, ny, nz),
        out_shape=jax.ShapeDtypeStruct(value_rows.shape, BF16),
        in_specs=[vmem] * 7,
        out_specs=vmem,
        scratch_shapes=[
            pltpu.VMEM((heads, D, 2 * D), F32),
            pltpu.VMEM((nz, D, 2 * D), F32),
            pltpu.VMEM((ny, D, 2 * D), F32),
            pltpu.VMEM((D, 2 * D), F32),
            pltpu.VMEM((nz, D, 2 * D), F32),
            pltpu.VMEM((nz, D, D), F32),
            pltpu.VMEM((heads, D, D), F32),
            pltpu.VMEM((heads, D, D), F32),
            pltpu.VMEM((heads, D, D), F32),
            pltpu.VMEM((D, D), F32),
            dma((heads,)),
            dma((nz,)),
            dma((ny,)),
            dma((ny,)),
            dma((nz,)),
            dma((heads,)),
        ],
        compiler_params=pltpu.CompilerParams(
            collective_id=0, has_side_effects=True, vmem_limit_bytes=48 * 2**20
        ),
        name="ctx_scan",
    )(
        queries,
        key_rows,
        value_rows,
        beta_logit.T,
        log_decay.T,
        out_gate,
        norm_gain[None],
    )
    return pl.pallas_call(
        functools.partial(head_kernel, n),
        out_shape=jax.ShapeDtypeStruct((tokens, width), BF16),
        in_specs=[vmem] * 2,
        out_specs=vmem,
        scratch_shapes=[
            pltpu.VMEM((n // 2, tokens, width), F32),
            pltpu.VMEM((n // 2, tokens, width), F32),
            pltpu.VMEM((n // 2, tokens, width), F32),
            pltpu.VMEM((n // 2, tokens, width), F32),
            dma((n // 2,)),
            dma((n // 2,)),
            dma((n // 2,)),
            dma((n // 2,)),
        ],
        compiler_params=pltpu.CompilerParams(
            collective_id=1, has_side_effects=True, vmem_limit_bytes=48 * 2**20
        ),
        name="head_sum",
    )(gated, out_weight)


def solution(mesh):
    return jax.shard_map(
        per_device,
        mesh=mesh,
        in_specs=(
            P("ctx", "head"),
            P("ctx", "head"),
            P("ctx", "head"),
            P("ctx", "head"),
            P("ctx", "head"),
            P("ctx", "head"),
            P(),
            P("head", None),
        ),
        out_specs=P("ctx", "head"),
        check_vma=False,
    )
```

```python
import functools

import jax
import jax.numpy as jnp
from jax import lax
from jax.experimental import pallas as pl
from jax.experimental.pallas import tpu as pltpu
from jax.sharding import PartitionSpec as P

MESH = pl.DeviceIdType.MESH
F32 = jnp.float32
BF16 = jnp.bfloat16
D = 128


def mm(a, b):
    batch = tuple(range(a.ndim - 2))
    dims = (((a.ndim - 1,), (b.ndim - 2,)), (batch, batch))
    return lax.dot_general(a, b, dims, precision=lax.Precision.HIGHEST, preferred_element_type=F32)


def mm_bf16(a, b):
    batch = tuple(range(a.ndim - 2))
    dims = (((a.ndim - 1,), (b.ndim - 2,)), (batch, batch))
    return lax.dot_general(a, b, dims, preferred_element_type=F32)


def mm_split(a, b):
    high = a.astype(BF16)
    low = (a - high.astype(F32)).astype(BF16)
    return mm_bf16(high, b) + mm_bf16(low, b)


def cut(a):
    high = a.astype(BF16)
    return high, (a - high.astype(F32)).astype(BF16)


def mm3(a, b):
    a_high, a_low = cut(a)
    b_high, b_low = cut(b)
    return mm_bf16(a_high, b_high) + (mm_bf16(a_high, b_low) + mm_bf16(a_low, b_high))


def nt(a, b):
    return lax.dot_general(
        a, b, (((1,), (1,)), ((), ())), precision=lax.Precision.HIGHEST, preferred_element_type=F32
    )


def iotas(n):
    return (
        lax.broadcasted_iota(jnp.int32, (n, n), 0),
        lax.broadcasted_iota(jnp.int32, (n, n), 1),
    )


def unit_lower_inverse(strict_part):
    row, col = iotas(D)
    eye = jnp.where(row == col, 1.0, 0.0).astype(F32)

    def off(half):
        shift = half.bit_length() - 1
        rb, cb = row >> shift, col >> shift
        mask = ((rb ^ cb) == 1) & (rb > cb)
        return jnp.where(mask[None], strict_part, 0.0)

    inverse = eye[None] - off(1)
    half = 2
    while half < D:
        inverse = inverse - mm(inverse, mm(off(half), inverse))
        half *= 2
    return inverse


def follow(out, later, earlier):
    both = mm3(later[0], jnp.concatenate([earlier[0], earlier[1]], axis=1))
    out[0] = both[:, :D]
    out[1] = both[:, D:] + later[1]


def kernel(
    ny,
    nz,
    n,
    q_hbm,
    k_hbm,
    v_hbm,
    beta_hbm,
    decay_hbm,
    gate_hbm,
    gain_hbm,
    weight_hbm,
    out_ref,
    q_ref,
    k_ref,
    v_ref,
    beta_ref,
    decay_ref,
    gate_ref,
    gain_ref,
    weight_ref,
    own,
    zin,
    yin,
    total_ref,
    tree,
    prefix,
    sout,
    sin,
    within,
    qmap,
    state_ref,
    gated_ref,
    pair_out,
    pair_in,
    mine,
    chip_in,
    load,
    zsend,
    zrecv,
    ysend,
    yrecv,
    rsend,
    rrecv,
    psend,
    precv,
    csend,
    crecv,
):
    heads = v_ref.shape[1] // D
    kheads = k_ref.shape[1] // D
    group = heads // kheads
    chips = n // 2
    width = out_ref.shape[1]
    slots = 2 * nz
    blocks = ny // 2
    ctx, head = lax.axis_index("ctx"), lax.axis_index("head")
    y, z = ctx // nz, ctx % nz
    x, core = head // 2, head % 2
    block, row_in = y // 2, y % 2
    place = row_in * nz + z
    sibling = x * 2 + 1 - core
    worker = (z % 2 == core) & (row_in == core)

    def at(other_block, other_row, other_z):
        return (other_block * 2 + other_row) * nz + other_z

    barrier = pltpu.get_barrier_semaphore()
    greeted = 0

    def greet(where):
        pl.semaphore_signal(barrier, inc=1, device_id=where, device_id_type=MESH)

    for dr in range(2):
        for dz in range(nz):
            if dr or dz:
                greet((at(block, (row_in + dr) % 2, (z + dz) % nz), head))
                greeted += 1
    for db in range(1, blocks):
        greet((at((block + db) % blocks, row_in, z), head))
        greeted += 1
    greet((ctx, sibling))
    for dx in range(1, chips):
        greet((ctx, ((x + dx) % chips) * 2 + core))
    greeted += chips

    loads = [
        pltpu.make_async_copy(src, dst, load.at[i])
        for i, (src, dst) in enumerate(
            [
                (k_hbm, k_ref),
                (decay_hbm, decay_ref),
                (beta_hbm, beta_ref),
                (v_hbm, v_ref),
                (q_hbm, q_ref),
                (gate_hbm, gate_ref),
                (gain_hbm, gain_ref),
                (weight_hbm, weight_ref),
            ]
        )
    ]
    for copy in loads:
        copy.start()
    for copy in loads[:5]:
        copy.wait()

    row, col = iotas(D)
    causal, strict = row >= col, row > col
    eye = jnp.where(row == col, 1.0, 0.0).astype(F32)
    tri = jnp.where(causal, 1.0, 0.0).astype(F32)
    keys = jnp.stack([k_ref[:, i * D : (i + 1) * D] for i in range(kheads)])
    queries = jnp.stack([q_ref[:, i * D : (i + 1) * D] for i in range(kheads)])
    values = jnp.stack([v_ref[:, i * D : (i + 1) * D] for i in range(heads)])
    keys32 = keys.astype(F32)
    keys_t32 = jnp.stack([keys32[i].T for i in range(kheads)])
    keys_t = keys_t32.astype(BF16)
    r_col = lax.rsqrt(jnp.sum(keys32 * keys32, axis=2, keepdims=True) + 1e-06)
    r_row = lax.rsqrt(jnp.sum(keys_t32 * keys_t32, axis=1, keepdims=True) + 1e-06)
    gram = mm_bf16(keys, keys_t) * (r_col * r_row)
    scores = mm_bf16(queries, keys_t) * r_row

    beta_row = jax.nn.sigmoid(beta_ref[...])
    decay_row = decay_ref[...]
    cum_row = nt(decay_row, tri)
    cum_col = nt(tri, decay_row)
    beta_col = nt(eye, beta_row)
    exp_row = jnp.exp(cum_row)
    exp_col = jnp.exp(cum_col)
    total = cum_row[:, D - 1 : D]
    exp_total = jnp.exp(total)
    tail_row = jnp.exp(total - cum_row)

    def per_head(fn):
        return jnp.stack([fn(h) for h in range(heads)])

    decay_mat = per_head(
        lambda h: jnp.exp(
            jnp.where(causal, cum_col[:, h : h + 1] - cum_row[h : h + 1, :], -1e30)
        )
    )
    strict_part = per_head(
        lambda h: jnp.where(
            strict, beta_col[:, h : h + 1] * gram[h // group] * decay_mat[h], 0.0
        )
    )
    inverse = unit_lower_inverse(strict_part)
    scaled = per_head(lambda h: inverse[h] * beta_row[h : h + 1, :])
    pseudo = mm_split(scaled, values)
    wy = mm_split(
        per_head(lambda h: scaled[h] * (exp_row[h : h + 1, :] * r_row[h // group])),
        per_head(lambda h: keys[h // group]),
    )
    wy_pseudo = jnp.concatenate([wy, pseudo], axis=2)
    tails = per_head(
        lambda h: keys_t32[h // group] * (r_row[h // group] * tail_row[h : h + 1, :])
    )
    moved = mm(tails, wy_pseudo)
    for h in range(heads):
        own[h, 0] = exp_total[h : h + 1, :] * eye - moved[h, :, :D]
        own[h, 1] = moved[h, :, D:]

    pl.semaphore_wait(barrier, greeted)

    def head_copy(k):
        h = (z // 2 + k) % heads
        return pltpu.make_async_remote_copy(
            src_ref=own.at[h],
            dst_ref=zin.at[place],
            send_sem=zsend.at[k],
            recv_sem=zrecv.at[place],
            device_id=(at(block, core, 2 * h + core), head),
            device_id_type=MESH,
        )

    by_distance = sorted(range(heads), key=lambda k: -min(k, heads - k))
    for k in by_distance:
        if k:
            head_copy(k).start()
        else:

            @pl.when(jnp.logical_not(worker))
            def _():
                head_copy(0).start()

            @pl.when(worker)
            def _():
                zin[pl.ds(place, 1)] = own[pl.ds(z // 2, 1)]

    mixed = mm3(per_head(lambda h: scores[h // group] * decay_mat[h]), wy_pseudo)
    for h in range(heads):
        within[h] = mixed[h, :, D:]
        qmap[h] = exp_col[:, h : h + 1] * queries[h // group].astype(F32) - mixed[h, :, :D]
    for copy in loads[5:]:
        copy.wait()

    def block_copy(target, state_only):
        src = total_ref.at[1] if state_only else total_ref
        dst = yin.at[block, 1] if state_only else yin.at[block]
        return pltpu.make_async_remote_copy(
            src_ref=src,
            dst_ref=dst,
            send_sem=ysend.at[target],
            recv_sem=yrecv.at[block],
            device_id=(at(target, row_in, z), head),
            device_id_type=MESH,
        )

    def each_block_copy(act):
        for target in range(blocks - 1, 0, -1):

            @pl.when(block == 0)
            def _():
                act(block_copy(target, True))

            @pl.when((block > 0) & (target > block))
            def _():
                act(block_copy(target, False))

    def state_copy(dr, dz):
        i = ((row_in + dr) % 2) * nz + (z + dz) % nz
        return pltpu.make_async_remote_copy(
            src_ref=sout.at[i],
            dst_ref=sin.at[z // 2],
            send_sem=rsend.at[dr * nz + dz],
            recv_sem=rrecv.at[z // 2],
            device_id=(at(block, (row_in + dr) % 2, (z + dz) % nz), head),
            device_id_type=MESH,
        )

    def arrived(dst, sem):
        pltpu.make_async_remote_copy(
            src_ref=dst,
            dst_ref=dst,
            send_sem=zsend.at[0],
            recv_sem=sem,
            device_id=(ctx, sibling),
            device_id_type=MESH,
        ).wait_recv()

    targets = [
        (dr, dz)
        for dz in sorted(range(nz), key=lambda d: -min(d, nz - d))
        for dr in (1, 0)
    ]

    @pl.when(worker)
    def _():
        node = {}
        used = 0

        def spot(low, high):
            nonlocal used
            if high - low == 1:
                return zin.at[low]
            if (low, high) == (0, slots):
                return total_ref
            if low == 0:
                return prefix.at[high]
            used += 1
            return tree.at[used - 1]

        for i in range(slots):

            @pl.when(place != i)
            def _():
                arrived(zin.at[i], zrecv.at[i])

            node[(i, i + 1)] = spot(i, i + 1)
            if i == 0:
                prefix[1] = zin[0]
            low, high, span = i, i + 1, 1
            while high % (2 * span) == 0 and 2 * span <= slots:
                out = spot(high - 2 * span, high)
                follow(out, node[(low, high)], node[(low - span, low)])
                low, span = low - span, 2 * span
                node[(low, high)] = out
        each_block_copy(lambda copy: copy.start())
        prefix[0, 0] = eye
        prefix[0, 1] = jnp.zeros((D, D), F32)
        for i in range(3, slots):
            step = i & -i
            if step != i:
                follow(prefix.at[i], node[(i - step, i)], prefix.at[i - step])

        @pl.when(block == 0)
        def _():
            state_ref[...] = jnp.zeros((D, D), F32)

        @pl.when(block > 0)
        def _():
            arrived(yin.at[0, 1], yrecv.at[0])
            state_ref[...] = yin[0, 1]

        for i in range(1, blocks - 1):

            @pl.when(i < block)
            def _():
                arrived(yin.at[i], yrecv.at[i])
                state_ref[...] = mm3(yin[i, 0], state_ref[...]) + yin[i, 1]

        state = state_ref[...]
        for dr, dz in targets:
            i = ((row_in + dr) % 2) * nz + (z + dz) % nz
            block_in = prefix[pl.ds(i, 1)][0]
            result = mm3(block_in[0], state) + block_in[1]
            if dr or dz:
                sout[pl.ds(i, 1)] = result[None]
                state_copy(dr, dz).start()
            else:
                sin[pl.ds(z // 2, 1)] = result[None]

    for h in range(heads):

        @pl.when(jnp.logical_not(worker) | (z // 2 != h))
        def _():
            arrived(sin.at[h], rrecv.at[h])

        core_out = within[h] + mm3(qmap[h], sin[h])
        normed = core_out * lax.rsqrt(jnp.mean(core_out * core_out, axis=1, keepdims=True) + 1e-06)
        gate = gate_ref[:, h * D : (h + 1) * D].astype(F32)
        gated_ref[:, h * D : (h + 1) * D] = (
            normed * gain_ref[...] * (gate / (1.0 + jnp.exp(-gate)))
        ).astype(BF16)

    gated = gated_ref[...]

    def columns(chip, which):
        start = pl.multiple_of((chip * 2 + which) * width, width)
        return mm_bf16(gated, weight_ref[:, pl.ds(start, width)])

    def pair_copy(step):
        return pltpu.make_async_remote_copy(
            src_ref=pair_out.at[step],
            dst_ref=pair_in.at[step],
            send_sem=psend.at[step],
            recv_sem=precv.at[step],
            device_id=(ctx, sibling),
            device_id_type=MESH,
        )

    def chip_copy(step):
        return pltpu.make_async_remote_copy(
            src_ref=mine.at[step],
            dst_ref=chip_in.at[step],
            send_sem=csend.at[step],
            recv_sem=crecv.at[step],
            device_id=(ctx, ((x + step) % chips) * 2 + core),
            device_id_type=MESH,
        )

    order = sorted(range(chips), key=lambda s: -min(s, chips - s))
    for step in order:
        pair_out[step] = columns((x + step) % chips, 1 - core)
        pair_copy(step).start()
    for step in order:
        mine[step] = columns((x + step) % chips, core)
    for step in order:
        pair_copy(step).wait_recv()
        mine[step] = mine[step] + pair_in[step]
        if step:
            chip_copy(step).start()
    summed = mine[0]
    for step in order[1:-1] + order[:-1][:1]:
        chip_copy(step).wait_recv()
        summed = summed + chip_in[step]
    out_ref[...] = summed.astype(BF16)

    for k in range(heads):
        if k:
            head_copy(k).wait_send()
        else:

            @pl.when(jnp.logical_not(worker))
            def _():
                head_copy(0).wait_send()

    @pl.when(worker)
    def _():
        each_block_copy(lambda copy: copy.wait_send())
        for dr, dz in targets:
            if dr or dz:
                state_copy(dr, dz).wait_send()

    for step in order:
        pair_copy(step).wait_send()
        if step:
            chip_copy(step).wait_send()


def per_device(
    queries, key_rows, value_rows, beta_logit, log_decay, out_gate, norm_gain, out_weight
):
    heads = value_rows.shape[1] // D
    tokens = value_rows.shape[0]
    nz = 2 * heads
    ny = lax.axis_size("ctx") // nz
    n = lax.axis_size("head")
    width = out_weight.shape[1] // n
    vmem = pltpu.VMEM
    dma = pltpu.SemaphoreType.DMA
    args = (
        queries,
        key_rows,
        value_rows,
        beta_logit.T,
        log_decay.T,
        out_gate,
        norm_gain[None],
        out_weight,
    )
    return pl.pallas_call(
        functools.partial(kernel, ny, nz, n),
        out_shape=jax.ShapeDtypeStruct((tokens, width), BF16),
        in_specs=[pl.BlockSpec(memory_space=pltpu.HBM)] * len(args),
        out_specs=pl.BlockSpec(memory_space=vmem),
        scratch_shapes=[vmem(a.shape, a.dtype) for a in args]
        + [
            vmem((heads, 2, D, D), F32),
            vmem((2 * nz, 2, D, D), F32),
            vmem((ny // 2, 2, D, D), F32),
            vmem((2, D, D), F32),
            vmem((2 * nz, 2, D, D), F32),
            vmem((2 * nz, 2, D, D), F32),
            vmem((2 * nz, D, D), F32),
            vmem((heads, D, D), F32),
            vmem((heads, D, D), F32),
            vmem((heads, D, D), F32),
            vmem((D, D), F32),
            vmem((tokens, heads * D), BF16),
            vmem((n // 2, tokens, width), F32),
            vmem((n // 2, tokens, width), F32),
            vmem((n // 2, tokens, width), F32),
            vmem((n // 2, tokens, width), F32),
            dma((len(args),)),
            dma((heads,)),
            dma((2 * nz,)),
            dma((ny // 2,)),
            dma((ny // 2,)),
            dma((2 * nz,)),
            dma((heads,)),
            dma((n // 2,)),
            dma((n // 2,)),
            dma((n // 2,)),
            dma((n // 2,)),
        ],
        compiler_params=pltpu.CompilerParams(
            collective_id=0, has_side_effects=True, vmem_limit_bytes=56 * 2**20
        ),
        name="delta_layer",
    )(*args)


def solution(mesh):
    return jax.shard_map(
        per_device,
        mesh=mesh,
        in_specs=(
            P("ctx", "head"),
            P("ctx", "head"),
            P("ctx", "head"),
            P("ctx", "head"),
            P("ctx", "head"),
            P("ctx", "head"),
            P(),
            P("head", None),
        ),
        out_specs=P("ctx", "head"),
        check_vma=False,
    )
```

```python
import functools

import jax
import jax.numpy as jnp
from jax import lax
from jax.experimental import pallas as pl
from jax.experimental.pallas import tpu as pltpu
from jax.sharding import PartitionSpec as P

MESH = pl.DeviceIdType.MESH
F32 = jnp.float32
BF16 = jnp.bfloat16
D = 128


def mm(a, b):
    batch = tuple(range(a.ndim - 2))
    dims = (((a.ndim - 1,), (b.ndim - 2,)), (batch, batch))
    return lax.dot_general(a, b, dims, precision=lax.Precision.HIGHEST, preferred_element_type=F32)


def mm_bf16(a, b):
    batch = tuple(range(a.ndim - 2))
    dims = (((a.ndim - 1,), (b.ndim - 2,)), (batch, batch))
    return lax.dot_general(a, b, dims, preferred_element_type=F32)


def mm_split(a, b):
    high = a.astype(BF16)
    low = (a - high.astype(F32)).astype(BF16)
    return mm_bf16(high, b) + mm_bf16(low, b)


def cut(a):
    high = a.astype(BF16)
    return high, (a - high.astype(F32)).astype(BF16)


def mm3(a, b):
    a_high, a_low = cut(a)
    b_high, b_low = cut(b)
    return mm_bf16(a_high, b_high) + (mm_bf16(a_high, b_low) + mm_bf16(a_low, b_high))


def nt(a, b):
    return lax.dot_general(
        a, b, (((1,), (1,)), ((), ())), precision=lax.Precision.HIGHEST, preferred_element_type=F32
    )


def iotas(n):
    return (
        lax.broadcasted_iota(jnp.int32, (n, n), 0),
        lax.broadcasted_iota(jnp.int32, (n, n), 1),
    )


def unit_lower_inverse(strict_part):
    row, col = iotas(D)
    eye = jnp.where(row == col, 1.0, 0.0).astype(F32)

    def off(half):
        shift = half.bit_length() - 1
        rb, cb = row >> shift, col >> shift
        mask = ((rb ^ cb) == 1) & (rb > cb)
        return jnp.where(mask[None], strict_part, 0.0)

    inverse = eye[None] - off(1)
    half = 2
    while half < D:
        inverse = inverse - mm(inverse, mm(off(half), inverse))
        half *= 2
    return inverse


def kernel(
    ny,
    nz,
    n,
    q_hbm,
    k_hbm,
    v_hbm,
    beta_hbm,
    decay_hbm,
    gate_hbm,
    gain_hbm,
    weight_hbm,
    out_ref,
    q_ref,
    k_ref,
    v_ref,
    beta_ref,
    decay_ref,
    gate_ref,
    gain_ref,
    weight_ref,
    own_t,
    own_s,
    zin_t,
    zin_s,
    yin_t,
    yin_s,
    total_t,
    total_s,
    prefix_t,
    prefix_s,
    suffix,
    reach,
    sout,
    sin,
    within,
    qmap,
    gated_ref,
    pair_out,
    pair_in,
    mine,
    chip_in,
    load,
    zsend_t,
    zsend_s,
    zrecv_t,
    zrecv_s,
    ysend_t,
    ysend_s,
    yrecv_t,
    yrecv_s,
    rsend,
    rrecv,
    psend,
    precv,
    csend,
    crecv,
):
    heads = v_ref.shape[1] // D
    kheads = k_ref.shape[1] // D
    group = heads // kheads
    chips = n // 2
    width = out_ref.shape[1]
    ctx, head = lax.axis_index("ctx"), lax.axis_index("head")
    y, z = ctx // nz, ctx % nz
    x, core = head // 2, head % 2
    sibling = x * 2 + 1 - core
    worker = z % 2 == core

    barrier = pltpu.get_barrier_semaphore()

    def greet(where):
        pl.semaphore_signal(barrier, inc=1, device_id=where, device_id_type=MESH)

    for dz in range(1, nz):
        greet((y * nz + (z + dz) % nz, head))
    for dy in range(1, ny):
        greet((((y + dy) % ny) * nz + z, head))
    greet((ctx, sibling))
    for dx in range(1, chips):
        greet((ctx, ((x + dx) % chips) * 2 + core))
    greeted = nz - 1 + ny - 1 + chips

    loads = [
        pltpu.make_async_copy(src, dst, load.at[i])
        for i, (src, dst) in enumerate(
            [
                (k_hbm, k_ref),
                (decay_hbm, decay_ref),
                (beta_hbm, beta_ref),
                (v_hbm, v_ref),
                (q_hbm, q_ref),
                (gate_hbm, gate_ref),
                (gain_hbm, gain_ref),
                (weight_hbm, weight_ref),
            ]
        )
    ]
    for copy in loads:
        copy.start()
    for copy in loads[:5]:
        copy.wait()

    row, col = iotas(D)
    causal, strict = row >= col, row > col
    eye = jnp.where(row == col, 1.0, 0.0).astype(F32)
    tri = jnp.where(causal, 1.0, 0.0).astype(F32)
    keys = jnp.stack([k_ref[:, i * D : (i + 1) * D] for i in range(kheads)])
    queries = jnp.stack([q_ref[:, i * D : (i + 1) * D] for i in range(kheads)])
    values = jnp.stack([v_ref[:, i * D : (i + 1) * D] for i in range(heads)])
    keys32 = keys.astype(F32)
    keys_t32 = jnp.stack([keys32[i].T for i in range(kheads)])
    keys_t = keys_t32.astype(BF16)
    r_col = lax.rsqrt(jnp.sum(keys32 * keys32, axis=2, keepdims=True) + 1e-06)
    r_row = lax.rsqrt(jnp.sum(keys_t32 * keys_t32, axis=1, keepdims=True) + 1e-06)
    gram = mm_bf16(keys, keys_t) * (r_col * r_row)
    scores = mm_bf16(queries, keys_t) * r_row

    beta_row = jax.nn.sigmoid(beta_ref[...])
    decay_row = decay_ref[...]
    cum_row = nt(decay_row, tri)
    cum_col = nt(tri, decay_row)
    beta_col = nt(eye, beta_row)
    exp_row = jnp.exp(cum_row)
    exp_col = jnp.exp(cum_col)
    total = cum_row[:, D - 1 : D]
    exp_total = jnp.exp(total)
    tail_row = jnp.exp(total - cum_row)

    def per_head(fn):
        return jnp.stack([fn(h) for h in range(heads)])

    decay_mat = per_head(
        lambda h: jnp.exp(
            jnp.where(causal, cum_col[:, h : h + 1] - cum_row[h : h + 1, :], -1e30)
        )
    )
    strict_part = per_head(
        lambda h: jnp.where(
            strict, beta_col[:, h : h + 1] * gram[h // group] * decay_mat[h], 0.0
        )
    )
    inverse = unit_lower_inverse(strict_part)
    scaled = per_head(lambda h: inverse[h] * beta_row[h : h + 1, :])
    pseudo = mm_split(scaled, values)
    wy = mm_split(
        per_head(lambda h: scaled[h] * (exp_row[h : h + 1, :] * r_row[h // group])),
        per_head(lambda h: keys[h // group]),
    )
    wy_pseudo = jnp.concatenate([wy, pseudo], axis=2)
    tails = per_head(
        lambda h: keys_t32[h // group] * (r_row[h // group] * tail_row[h : h + 1, :])
    )
    moved = mm(tails, wy_pseudo)
    for h in range(heads):
        own_t[h] = exp_total[h : h + 1, :] * eye - moved[h, :, :D]
        own_s[h] = moved[h, :, D:]

    pl.semaphore_wait(barrier, greeted)

    def head_copy(k, own, zin, send, recv):
        h = (z // 2 + k) % heads
        return pltpu.make_async_remote_copy(
            src_ref=own.at[h],
            dst_ref=zin.at[z],
            send_sem=send.at[k],
            recv_sem=recv.at[z],
            device_id=(y * nz + 2 * h + core, head),
            device_id_type=MESH,
        )

    moves = ((own_t, zin_t, zsend_t, zrecv_t), (own_s, zin_s, zsend_s, zrecv_s))
    by_distance = sorted(range(heads), key=lambda k: -min(k, heads - k))
    for move in moves:
        for k in by_distance:
            if k:
                head_copy(k, *move).start()
            else:

                @pl.when(jnp.logical_not(worker))
                def _():
                    head_copy(0, *move).start()

                @pl.when(worker)
                def _():
                    move[1][pl.ds(z, 1)] = move[0][pl.ds(z // 2, 1)]

    mixed = mm3(per_head(lambda h: scores[h // group] * decay_mat[h]), wy_pseudo)
    for h in range(heads):
        within[h] = mixed[h, :, D:]
        qmap[h] = exp_col[:, h : h + 1] * queries[h // group].astype(F32) - mixed[h, :, :D]
    for copy in loads[5:]:
        copy.wait()

    def row_copy(dy, src, yin, send, recv):
        return pltpu.make_async_remote_copy(
            src_ref=src,
            dst_ref=yin.at[dy],
            send_sem=send.at[dy],
            recv_sem=recv.at[dy],
            device_id=((y + dy) * nz + z, head),
            device_id_type=MESH,
        )

    far_rows = sorted(range(1, ny), key=lambda d: -min(d, ny - d))

    def each_row_t(act):
        for dy in far_rows:

            @pl.when((y > 0) & (y + dy < ny))
            def _():
                act(row_copy(dy, total_t, yin_t, ysend_t, yrecv_t))

    def each_row_s(act):
        for dy in far_rows:

            @pl.when(y + dy < ny)
            def _():
                act(row_copy(dy, total_s, yin_s, ysend_s, yrecv_s))

    def state_copy(dz):
        i = (z + dz) % nz
        return pltpu.make_async_remote_copy(
            src_ref=sout.at[i],
            dst_ref=sin.at[z // 2],
            send_sem=rsend.at[dz],
            recv_sem=rrecv.at[z // 2],
            device_id=(y * nz + i, head),
            device_id_type=MESH,
        )

    def arrived(dst, sem):
        pltpu.make_async_remote_copy(
            src_ref=dst,
            dst_ref=dst,
            send_sem=zsend_t.at[0],
            recv_sem=sem,
            device_id=(ctx, sibling),
            device_id_type=MESH,
        ).wait_recv()

    targets = sorted(range(nz), key=lambda d: -min(d, nz - d))

    @pl.when(worker)
    def _():
        def wait_place(zin, recv):
            for i in range(nz):

                @pl.when(z != i)
                def _():
                    arrived(zin.at[i], recv.at[i])

        wait_place(zin_t, zrecv_t)
        first = {(i, i + 1): zin_t[i] for i in range(nz)}

        def trans(low, high):
            if (low, high) not in first:
                span = 1 << ((high - low - 1).bit_length() - 1)
                middle = low + span if low % (2 * span) == 0 else high - span
                first[(low, high)] = mm3(trans(middle, high), trans(low, middle))
            return first[(low, high)]

        total_t[...] = trans(0, nz)
        each_row_t(lambda copy: copy.start())
        for i in range(1, nz):
            suffix[:, (i - 1) * D : i * D] = trans(i, nz)
        prefix_t[0] = eye
        for i in range(1, nz):
            prefix_t[i] = trans(0, i)

        wait_place(zin_s, zrecv_s)
        total_s[...] = zin_s[nz - 1] + mm3(
            suffix[...], zin_s[: nz - 1].reshape((nz - 1) * D, D)
        )
        each_row_s(lambda copy: copy.start())

        prefix_s[0] = jnp.zeros((D, D), F32)
        states = {(i, i + 1): zin_s[i] for i in range(nz)}

        def state_of(low, high):
            if (low, high) not in states:
                span = 1 << ((high - low - 1).bit_length() - 1)
                middle = low + span if low % (2 * span) == 0 else high - span
                states[(low, high)] = mm3(trans(middle, high), state_of(low, middle)) + state_of(
                    middle, high
                )
            return states[(low, high)]

        for i in range(1, nz):
            prefix_s[i] = state_of(0, i)

        reach[:, :D] = eye
        for dy in range(2, ny):
            here = slice((dy - 1) * D, dy * D)
            before = slice((dy - 2) * D, (dy - 1) * D)

            @pl.when(dy <= y)
            def _():
                arrived(yin_t.at[dy - 1], yrecv_t.at[dy - 1])
                if dy == 2:
                    reach[:, here] = yin_t[1]
                else:
                    reach[:, here] = mm3(reach[:, before], yin_t[dy - 1])

            @pl.when(dy > y)
            def _():
                reach[:, here] = jnp.zeros((D, D), F32)

        for dy in range(1, ny):

            @pl.when(dy <= y)
            def _():
                arrived(yin_s.at[dy], yrecv_s.at[dy])

            @pl.when(dy > y)
            def _():
                yin_s[dy] = jnp.zeros((D, D), F32)

        state = mm3(reach[...], yin_s[1:].reshape((ny - 1) * D, D))
        for dz in targets:
            i = (z + dz) % nz
            result = mm3(prefix_t[pl.ds(i, 1)][0], state) + prefix_s[pl.ds(i, 1)][0]
            if dz:
                sout[pl.ds(i, 1)] = result[None]
                state_copy(dz).start()
            else:
                sin[pl.ds(z // 2, 1)] = result[None]

    for h in range(heads):

        @pl.when(jnp.logical_not(worker) | (z // 2 != h))
        def _():
            arrived(sin.at[h], rrecv.at[h])

        core_out = within[h] + mm3(qmap[h], sin[h])
        normed = core_out * lax.rsqrt(jnp.mean(core_out * core_out, axis=1, keepdims=True) + 1e-06)
        gate = gate_ref[:, h * D : (h + 1) * D].astype(F32)
        gated_ref[:, h * D : (h + 1) * D] = (
            normed * gain_ref[...] * (gate / (1.0 + jnp.exp(-gate)))
        ).astype(BF16)

    gated = gated_ref[...]

    def columns(chip, which):
        start = pl.multiple_of((chip * 2 + which) * width, width)
        return mm_bf16(gated, weight_ref[:, pl.ds(start, width)])

    def pair_copy(step):
        return pltpu.make_async_remote_copy(
            src_ref=pair_out.at[step],
            dst_ref=pair_in.at[step],
            send_sem=psend.at[step],
            recv_sem=precv.at[step],
            device_id=(ctx, sibling),
            device_id_type=MESH,
        )

    def chip_copy(step):
        return pltpu.make_async_remote_copy(
            src_ref=mine.at[step],
            dst_ref=chip_in.at[step],
            send_sem=csend.at[step],
            recv_sem=crecv.at[step],
            device_id=(ctx, ((x + step) % chips) * 2 + core),
            device_id_type=MESH,
        )

    order = sorted(range(chips), key=lambda s: -min(s, chips - s))
    for step in order:
        pair_out[step] = columns((x + step) % chips, 1 - core)
        pair_copy(step).start()
    for step in order:
        mine[step] = columns((x + step) % chips, core)
    for step in order:
        pair_copy(step).wait_recv()
        mine[step] = mine[step] + pair_in[step]
        if step:
            chip_copy(step).start()
    summed = mine[0]
    for step in order[1:-1] + order[:-1][:1]:
        chip_copy(step).wait_recv()
        summed = summed + chip_in[step]
    out_ref[...] = summed.astype(BF16)

    for move in moves:
        for k in range(heads):
            if k:
                head_copy(k, *move).wait_send()
            else:

                @pl.when(jnp.logical_not(worker))
                def _():
                    head_copy(0, *move).wait_send()

    @pl.when(worker)
    def _():
        each_row_t(lambda copy: copy.wait_send())
        each_row_s(lambda copy: copy.wait_send())
        for dz in targets:
            if dz:
                state_copy(dz).wait_send()

    for step in order:
        pair_copy(step).wait_send()
        if step:
            chip_copy(step).wait_send()


def per_device(
    queries, key_rows, value_rows, beta_logit, log_decay, out_gate, norm_gain, out_weight
):
    heads = value_rows.shape[1] // D
    tokens = value_rows.shape[0]
    nz = 2 * heads
    ny = lax.axis_size("ctx") // nz
    n = lax.axis_size("head")
    width = out_weight.shape[1] // n
    vmem = pltpu.VMEM
    dma = pltpu.SemaphoreType.DMA
    args = (
        queries,
        key_rows,
        value_rows,
        beta_logit.T,
        log_decay.T,
        out_gate,
        norm_gain[None],
        out_weight,
    )
    return pl.pallas_call(
        functools.partial(kernel, ny, nz, n),
        out_shape=jax.ShapeDtypeStruct((tokens, width), BF16),
        in_specs=[pl.BlockSpec(memory_space=pltpu.HBM)] * len(args),
        out_specs=pl.BlockSpec(memory_space=vmem),
        scratch_shapes=[vmem(a.shape, a.dtype) for a in args]
        + [
            vmem((heads, D, D), F32),
            vmem((heads, D, D), F32),
            vmem((nz, D, D), F32),
            vmem((nz, D, D), F32),
            vmem((ny, D, D), F32),
            vmem((ny, D, D), F32),
            vmem((D, D), F32),
            vmem((D, D), F32),
            vmem((nz, D, D), F32),
            vmem((nz, D, D), F32),
            vmem((D, (nz - 1) * D), F32),
            vmem((D, (ny - 1) * D), F32),
            vmem((nz, D, D), F32),
            vmem((heads, D, D), F32),
            vmem((heads, D, D), F32),
            vmem((heads, D, D), F32),
            vmem((tokens, heads * D), BF16),
            vmem((n // 2, tokens, width), F32),
            vmem((n // 2, tokens, width), F32),
            vmem((n // 2, tokens, width), F32),
            vmem((n // 2, tokens, width), F32),
            dma((len(args),)),
            dma((heads,)),
            dma((heads,)),
            dma((nz,)),
            dma((nz,)),
            dma((ny,)),
            dma((ny,)),
            dma((ny,)),
            dma((ny,)),
            dma((nz,)),
            dma((heads,)),
            dma((n // 2,)),
            dma((n // 2,)),
            dma((n // 2,)),
            dma((n // 2,)),
        ],
        compiler_params=pltpu.CompilerParams(
            collective_id=0, has_side_effects=True, vmem_limit_bytes=56 * 2**20
        ),
        name="delta_layer",
    )(*args)


def solution(mesh):
    return jax.shard_map(
        per_device,
        mesh=mesh,
        in_specs=(
            P("ctx", "head"),
            P("ctx", "head"),
            P("ctx", "head"),
            P("ctx", "head"),
            P("ctx", "head"),
            P("ctx", "head"),
            P(),
            P("head", None),
        ),
        out_specs=P("ctx", "head"),
        check_vma=False,
    )
```

```python
import functools

import jax
import jax.numpy as jnp
from jax import lax
from jax.experimental import pallas as pl
from jax.experimental.pallas import tpu as pltpu
from jax.sharding import PartitionSpec as P

MESH = pl.DeviceIdType.MESH
F32 = jnp.float32
BF16 = jnp.bfloat16
D = 128


def mm(a, b):
    batch = tuple(range(a.ndim - 2))
    dims = (((a.ndim - 1,), (b.ndim - 2,)), (batch, batch))
    return lax.dot_general(a, b, dims, precision=lax.Precision.HIGHEST, preferred_element_type=F32)


def mm_bf16(a, b):
    batch = tuple(range(a.ndim - 2))
    dims = (((a.ndim - 1,), (b.ndim - 2,)), (batch, batch))
    return lax.dot_general(a, b, dims, preferred_element_type=F32)


def mm_split(a, b):
    high = a.astype(BF16)
    low = (a - high.astype(F32)).astype(BF16)
    return mm_bf16(high, b) + mm_bf16(low, b)


def cut(a):
    high = a.astype(BF16)
    return high, (a - high.astype(F32)).astype(BF16)


def mm3(a, b):
    a_high, a_low = cut(a)
    b_high, b_low = cut(b)
    return mm_bf16(a_high, b_high) + (mm_bf16(a_high, b_low) + mm_bf16(a_low, b_high))


def nt(a, b):
    return lax.dot_general(
        a, b, (((1,), (1,)), ((), ())), precision=lax.Precision.HIGHEST, preferred_element_type=F32
    )


def iotas(n):
    return (
        lax.broadcasted_iota(jnp.int32, (n, n), 0),
        lax.broadcasted_iota(jnp.int32, (n, n), 1),
    )


def unit_lower_inverse(strict_part):
    row, col = iotas(D)
    eye = jnp.where(row == col, 1.0, 0.0).astype(F32)

    def off(half):
        shift = half.bit_length() - 1
        rb, cb = row >> shift, col >> shift
        mask = ((rb ^ cb) == 1) & (rb > cb)
        return jnp.where(mask[None], strict_part, 0.0)

    inverse = eye[None] - off(1)
    half = 2
    while half < D:
        inverse = inverse - mm3(inverse, mm3(off(half), inverse))
        half *= 2
    return inverse


def kernel(
    ny,
    nz,
    n,
    q_hbm,
    k_hbm,
    v_hbm,
    beta_hbm,
    decay_hbm,
    gate_hbm,
    gain_hbm,
    weight_hbm,
    out_ref,
    q_ref,
    k_ref,
    v_ref,
    beta_ref,
    decay_ref,
    gate_ref,
    gain_ref,
    weight_ref,
    own_t,
    own_s,
    zin_t,
    zin_s,
    yin_t,
    yin_s,
    total_t,
    total_s,
    prefix_t,
    prefix_s,
    suffix,
    reach,
    sout,
    sin,
    within,
    qmap,
    gating,
    gated_ref,
    pair_out,
    pair_in,
    mine,
    chip_in,
    ready,
    load,
    zsend_t,
    zsend_s,
    zrecv_t,
    zrecv_s,
    ysend_t,
    ysend_s,
    yrecv_t,
    yrecv_s,
    rsend,
    rrecv,
    psend,
    precv,
    csend,
    crecv,
):
    heads = v_ref.shape[1] // D
    kheads = k_ref.shape[1] // D
    group = heads // kheads
    chips = n // 2
    width = out_ref.shape[1]
    ctx, head = lax.axis_index("ctx"), lax.axis_index("head")
    y, z = ctx // nz, ctx % nz
    x, core = head // 2, head % 2
    sibling = x * 2 + 1 - core
    worker = z % 2 == core

    loads = [
        pltpu.make_async_copy(src, dst, load.at[i])
        for i, (src, dst) in enumerate(
            [
                (k_hbm, k_ref),
                (decay_hbm, decay_ref),
                (beta_hbm, beta_ref),
                (v_hbm, v_ref),
                (q_hbm, q_ref),
                (gate_hbm, gate_ref),
                (gain_hbm, gain_ref),
                (weight_hbm, weight_ref),
            ]
        )
    ]
    for copy in loads:
        copy.start()

    barrier = pltpu.get_barrier_semaphore()

    def greet(where):
        pl.semaphore_signal(barrier, inc=1, device_id=where, device_id_type=MESH)

    for other in range(1, nz):

        @pl.when(other > z)
        def _():
            greet((y * nz + other, head))

    for other in range(ny - 1):

        @pl.when(other < y)
        def _():
            greet((other * nz + z, head))

    greet((ctx, sibling))
    for dx in range(1, chips):
        greet((ctx, ((x + dx) % chips) * 2 + core))

    for copy in loads[:3]:
        copy.wait()

    row, col = iotas(D)
    causal, strict = row >= col, row > col
    eye = jnp.where(row == col, 1.0, 0.0).astype(F32)
    tri = jnp.where(causal, 1.0, 0.0).astype(F32)
    keys = jnp.stack([k_ref[:, i * D : (i + 1) * D] for i in range(kheads)])
    keys32 = keys.astype(F32)
    keys_t32 = jnp.stack([keys32[i].T for i in range(kheads)])
    keys_t = keys_t32.astype(BF16)
    r_col = lax.rsqrt(jnp.sum(keys32 * keys32, axis=2, keepdims=True) + 1e-06)
    r_row = lax.rsqrt(jnp.sum(keys_t32 * keys_t32, axis=1, keepdims=True) + 1e-06)
    gram = mm_bf16(keys, keys_t) * (r_col * r_row)

    beta_row = jax.nn.sigmoid(beta_ref[...])
    decay_row = decay_ref[...]
    cum_row = nt(decay_row, tri)
    cum_col = nt(tri, decay_row)
    beta_col = nt(eye, beta_row)
    exp_row = jnp.exp(cum_row)
    total = cum_row[:, D - 1 : D]
    exp_total = jnp.exp(total)
    tail_row = jnp.exp(total - cum_row)

    def per_head(fn):
        return jnp.stack([fn(h) for h in range(heads)])

    decay_mat = per_head(
        lambda h: jnp.exp(
            jnp.where(causal, cum_col[:, h : h + 1] - cum_row[h : h + 1, :], -1e30)
        )
    )
    strict_part = per_head(
        lambda h: jnp.where(
            strict, beta_col[:, h : h + 1] * gram[h // group] * decay_mat[h], 0.0
        )
    )
    pl.semaphore_wait(barrier, z + (ny - 1 - y) + chips)
    for other in range(nz - 1):

        @pl.when(other < z)
        def _():
            pl.semaphore_signal(
                ready.at[z], inc=1, device_id=(y * nz + other, head), device_id_type=MESH
            )

    inverse = unit_lower_inverse(strict_part)
    scaled = per_head(lambda h: inverse[h] * beta_row[h : h + 1, :])
    wy = mm_split(
        per_head(lambda h: scaled[h] * (exp_row[h : h + 1, :] * r_row[h // group])),
        per_head(lambda h: keys[h // group]),
    )
    tails = per_head(
        lambda h: keys_t32[h // group] * (r_row[h // group] * tail_row[h : h + 1, :])
    )
    moved = mm3(tails, wy)
    for h in range(heads):
        own_t[h] = exp_total[h : h + 1, :] * eye - moved[h]

    def head_copy(h, own, zin, send, recv):
        return pltpu.make_async_remote_copy(
            src_ref=own.at[h],
            dst_ref=zin.at[z],
            send_sem=send.at[h],
            recv_sem=recv.at[z],
            device_id=(y * nz + 2 * h + core, head),
            device_id_type=MESH,
        )

    move_t = (own_t, zin_t, zsend_t, zrecv_t)
    move_s = (own_s, zin_s, zsend_s, zrecv_s)

    def send_head(h, move):
        @pl.when(z != 2 * h + core)
        def _():
            head_copy(h, *move).start()

        @pl.when(z == 2 * h + core)
        def _():
            move[1][pl.ds(z, 1)] = move[0][h : h + 1]

    def await_ready(h):
        for other in (2 * h, 2 * h + 1):

            @pl.when(other > z)
            def _():
                pl.semaphore_wait(ready.at[other], 1)

    early = heads // 2
    for h in range(early):
        await_ready(h)
        send_head(h, move_t)
    loads[3].wait()
    values = jnp.stack([v_ref[:, i * D : (i + 1) * D] for i in range(heads)])
    pseudo = mm_split(scaled, values)
    gained = mm3(tails, pseudo)
    for h in range(heads):
        own_s[h] = gained[h]
    for h in range(early):
        send_head(h, move_s)
    for h in range(early, heads):
        await_ready(h)
        send_head(h, move_t)
        send_head(h, move_s)

    loads[4].wait()
    queries = jnp.stack([q_ref[:, i * D : (i + 1) * D] for i in range(kheads)])
    scores = mm_bf16(queries, keys_t) * r_row
    exp_col = jnp.exp(cum_col)
    wy_pseudo = jnp.concatenate([wy, pseudo], axis=2)
    mixed = mm3(per_head(lambda h: scores[h // group] * decay_mat[h]), wy_pseudo)
    for h in range(heads):
        within[h] = mixed[h, :, D:]
        qmap[h] = exp_col[:, h : h + 1] * queries[h // group].astype(F32) - mixed[h, :, :D]
    for copy in loads[5:]:
        copy.wait()
    for h in range(heads):
        gate = gate_ref[:, h * D : (h + 1) * D].astype(F32)
        gating[h] = gain_ref[...] * (gate / (1.0 + jnp.exp(-gate)))

    def row_copy(dy, src, yin, send, recv):
        return pltpu.make_async_remote_copy(
            src_ref=src,
            dst_ref=yin.at[dy],
            send_sem=send.at[dy],
            recv_sem=recv.at[dy],
            device_id=((y + dy) * nz + z, head),
            device_id_type=MESH,
        )

    far_rows = sorted(range(1, ny), key=lambda d: -min(d, ny - d))

    def each_row_t(act):
        for dy in far_rows:

            @pl.when((y > 0) & (y + dy < ny))
            def _():
                act(row_copy(dy, total_t, yin_t, ysend_t, yrecv_t))

    def each_row_s(act):
        for dy in far_rows:

            @pl.when(y + dy < ny)
            def _():
                act(row_copy(dy, total_s, yin_s, ysend_s, yrecv_s))

    def state_copy(dz):
        i = (z + dz) % nz
        return pltpu.make_async_remote_copy(
            src_ref=sout.at[i],
            dst_ref=sin.at[z // 2],
            send_sem=rsend.at[dz],
            recv_sem=rrecv.at[z // 2],
            device_id=(y * nz + i, head),
            device_id_type=MESH,
        )

    def arrived(dst, sem):
        pltpu.make_async_remote_copy(
            src_ref=dst,
            dst_ref=dst,
            send_sem=zsend_t.at[0],
            recv_sem=sem,
            device_id=(ctx, sibling),
            device_id_type=MESH,
        ).wait_recv()

    targets = sorted(range(nz), key=lambda d: -min(d, nz - d))

    @pl.when(worker)
    def _():
        def wait_place(zin, recv):
            for i in range(nz):

                @pl.when(z != i)
                def _():
                    arrived(zin.at[i], recv.at[i])

        wait_place(zin_t, zrecv_t)
        first = {(i, i + 1): zin_t[i] for i in range(nz)}

        def trans(low, high):
            if (low, high) not in first:
                span = 1 << ((high - low - 1).bit_length() - 1)
                middle = low + span if low % (2 * span) == 0 else high - span
                first[(low, high)] = mm3(trans(middle, high), trans(low, middle))
            return first[(low, high)]

        total_t[...] = trans(0, nz)
        each_row_t(lambda copy: copy.start())
        for i in range(1, nz):
            suffix[:, (i - 1) * D : i * D] = trans(i, nz)
        prefix_t[0] = eye
        for i in range(1, nz):
            prefix_t[i] = trans(0, i)

        wait_place(zin_s, zrecv_s)
        total_s[...] = zin_s[nz - 1] + mm3(
            suffix[...], zin_s[: nz - 1].reshape((nz - 1) * D, D)
        )
        each_row_s(lambda copy: copy.start())

        prefix_s[0] = jnp.zeros((D, D), F32)
        states = {(i, i + 1): zin_s[i] for i in range(nz)}

        def state_of(low, high):
            if (low, high) not in states:
                span = 1 << ((high - low - 1).bit_length() - 1)
                middle = low + span if low % (2 * span) == 0 else high - span
                states[(low, high)] = mm3(trans(middle, high), state_of(low, middle)) + state_of(
                    middle, high
                )
            return states[(low, high)]

        for i in range(1, nz):
            prefix_s[i] = state_of(0, i)

        reach[:, :D] = eye
        for dy in range(2, ny):
            here = slice((dy - 1) * D, dy * D)
            before = slice((dy - 2) * D, (dy - 1) * D)

            @pl.when(dy <= y)
            def _():
                arrived(yin_t.at[dy - 1], yrecv_t.at[dy - 1])
                if dy == 2:
                    reach[:, here] = yin_t[1]
                else:
                    reach[:, here] = mm3(reach[:, before], yin_t[dy - 1])

            @pl.when(dy > y)
            def _():
                reach[:, here] = jnp.zeros((D, D), F32)

        for dy in range(1, ny):

            @pl.when(dy <= y)
            def _():
                arrived(yin_s.at[dy], yrecv_s.at[dy])

            @pl.when(dy > y)
            def _():
                yin_s[dy] = jnp.zeros((D, D), F32)

        state = mm3(reach[...], yin_s[1:].reshape((ny - 1) * D, D))
        for dz in targets:
            i = (z + dz) % nz
            result = mm3(prefix_t[pl.ds(i, 1)][0], state) + prefix_s[pl.ds(i, 1)][0]
            if dz:
                sout[pl.ds(i, 1)] = result[None]
                state_copy(dz).start()
            else:
                sin[pl.ds(z // 2, 1)] = result[None]

    for h in range(heads):

        @pl.when(jnp.logical_not(worker) | (z // 2 != h))
        def _():
            arrived(sin.at[h], rrecv.at[h])

    core_out = within[...] + mm3(qmap[...], sin[...])
    scale = lax.rsqrt(jnp.mean(core_out * core_out, axis=2, keepdims=True) + 1e-06)
    for h in range(heads):
        gated_ref[:, h * D : (h + 1) * D] = (core_out[h] * scale[h] * gating[h]).astype(BF16)

    gated = gated_ref[...]

    def columns(chip, which):
        start = pl.multiple_of((chip * 2 + which) * width, width)
        return mm_bf16(gated, weight_ref[:, pl.ds(start, width)])

    def pair_copy(step):
        return pltpu.make_async_remote_copy(
            src_ref=pair_out.at[step],
            dst_ref=pair_in.at[step],
            send_sem=psend.at[step],
            recv_sem=precv.at[step],
            device_id=(ctx, sibling),
            device_id_type=MESH,
        )

    def chip_copy(step):
        return pltpu.make_async_remote_copy(
            src_ref=mine.at[step],
            dst_ref=chip_in.at[step],
            send_sem=csend.at[step],
            recv_sem=crecv.at[step],
            device_id=(ctx, ((x + step) % chips) * 2 + core),
            device_id_type=MESH,
        )

    order = sorted(range(chips), key=lambda s: -min(s, chips - s))
    for step in order:
        pair_out[step] = columns((x + step) % chips, 1 - core)
        pair_copy(step).start()
    for step in order:
        mine[step] = columns((x + step) % chips, core)
    for step in order:
        pair_copy(step).wait_recv()
        mine[step] = mine[step] + pair_in[step]
        if step:
            chip_copy(step).start()
    for move in (move_t, move_s):
        for h in range(heads):

            @pl.when(z != 2 * h + core)
            def _():
                head_copy(h, *move).wait_send()

    @pl.when(worker)
    def _():
        each_row_t(lambda copy: copy.wait_send())
        each_row_s(lambda copy: copy.wait_send())
        for dz in targets:
            if dz:
                state_copy(dz).wait_send()

    for step in order:
        pair_copy(step).wait_send()

    summed = mine[0]
    for step in order[1:-1] + order[:-1][:1]:
        chip_copy(step).wait_recv()
        summed = summed + chip_in[step]
    out_ref[...] = summed.astype(BF16)

    for step in order:
        if step:
            chip_copy(step).wait_send()


def per_device(
    queries, key_rows, value_rows, beta_logit, log_decay, out_gate, norm_gain, out_weight
):
    heads = value_rows.shape[1] // D
    tokens = value_rows.shape[0]
    nz = 2 * heads
    ny = lax.axis_size("ctx") // nz
    n = lax.axis_size("head")
    width = out_weight.shape[1] // n
    vmem = pltpu.VMEM
    dma = pltpu.SemaphoreType.DMA
    args = (
        queries,
        key_rows,
        value_rows,
        beta_logit.T,
        log_decay.T,
        out_gate,
        norm_gain[None],
        out_weight,
    )
    return pl.pallas_call(
        functools.partial(kernel, ny, nz, n),
        out_shape=jax.ShapeDtypeStruct((tokens, width), BF16),
        in_specs=[pl.BlockSpec(memory_space=pltpu.HBM)] * len(args),
        out_specs=pl.BlockSpec(memory_space=vmem),
        scratch_shapes=[vmem(a.shape, a.dtype) for a in args]
        + [
            vmem((heads, D, D), F32),
            vmem((heads, D, D), F32),
            vmem((nz, D, D), F32),
            vmem((nz, D, D), F32),
            vmem((ny, D, D), F32),
            vmem((ny, D, D), F32),
            vmem((D, D), F32),
            vmem((D, D), F32),
            vmem((nz, D, D), F32),
            vmem((nz, D, D), F32),
            vmem((D, (nz - 1) * D), F32),
            vmem((D, (ny - 1) * D), F32),
            vmem((nz, D, D), F32),
            vmem((heads, D, D), F32),
            vmem((heads, D, D), F32),
            vmem((heads, D, D), F32),
            vmem((heads, D, D), F32),
            vmem((tokens, heads * D), BF16),
            vmem((n // 2, tokens, width), F32),
            vmem((n // 2, tokens, width), F32),
            vmem((n // 2, tokens, width), F32),
            vmem((n // 2, tokens, width), F32),
            pltpu.SemaphoreType.REGULAR((nz,)),
            dma((len(args),)),
            dma((heads,)),
            dma((heads,)),
            dma((nz,)),
            dma((nz,)),
            dma((ny,)),
            dma((ny,)),
            dma((ny,)),
            dma((ny,)),
            dma((nz,)),
            dma((heads,)),
            dma((n // 2,)),
            dma((n // 2,)),
            dma((n // 2,)),
            dma((n // 2,)),
        ],
        compiler_params=pltpu.CompilerParams(
            collective_id=0, has_side_effects=True, vmem_limit_bytes=56 * 2**20
        ),
        name="delta_layer",
    )(*args)


def solution(mesh):
    return jax.shard_map(
        per_device,
        mesh=mesh,
        in_specs=(
            P("ctx", "head"),
            P("ctx", "head"),
            P("ctx", "head"),
            P("ctx", "head"),
            P("ctx", "head"),
            P("ctx", "head"),
            P(),
            P("head", None),
        ),
        out_specs=P("ctx", "head"),
        check_vma=False,
    )
```

```python
import functools

import jax
import jax.numpy as jnp
from jax import lax
from jax.experimental import pallas as pl
from jax.experimental.pallas import tpu as pltpu
from jax.sharding import PartitionSpec as P

MESH = pl.DeviceIdType.MESH
F32 = jnp.float32
BF16 = jnp.bfloat16
D = 128


def mm(a, b):
    batch = tuple(range(a.ndim - 2))
    dims = (((a.ndim - 1,), (b.ndim - 2,)), (batch, batch))
    return lax.dot_general(a, b, dims, precision=lax.Precision.HIGHEST, preferred_element_type=F32)


def mm_bf16(a, b):
    batch = tuple(range(a.ndim - 2))
    dims = (((a.ndim - 1,), (b.ndim - 2,)), (batch, batch))
    return lax.dot_general(a, b, dims, preferred_element_type=F32)


def mm_split(a, b):
    high = a.astype(BF16)
    low = (a - high.astype(F32)).astype(BF16)
    return mm_bf16(high, b) + mm_bf16(low, b)


def cut(a):
    high = a.astype(BF16)
    return high, (a - high.astype(F32)).astype(BF16)


def mm3(a, b):
    a_high, a_low = cut(a)
    b_high, b_low = cut(b)
    return mm_bf16(a_high, b_high) + (mm_bf16(a_high, b_low) + mm_bf16(a_low, b_high))


def nt(a, b):
    return lax.dot_general(
        a, b, (((1,), (1,)), ((), ())), precision=lax.Precision.HIGHEST, preferred_element_type=F32
    )


def iotas(n):
    return (
        lax.broadcasted_iota(jnp.int32, (n, n), 0),
        lax.broadcasted_iota(jnp.int32, (n, n), 1),
    )


def unit_lower_inverse(strict_part):
    row, col = iotas(D)
    eye = jnp.where(row == col, 1.0, 0.0).astype(F32)

    def off(half):
        shift = half.bit_length() - 1
        rb, cb = row >> shift, col >> shift
        mask = ((rb ^ cb) == 1) & (rb > cb)
        return jnp.where(mask[None], strict_part, 0.0)

    inverse = eye[None] - off(1)
    half = 2
    while half < D:
        inverse = inverse - mm3(inverse, mm3(off(half), inverse))
        half *= 2
    return inverse


def kernel(
    ny,
    nz,
    n,
    q_hbm,
    k_hbm,
    v_hbm,
    beta_hbm,
    decay_hbm,
    gate_hbm,
    gain_hbm,
    weight_hbm,
    out_ref,
    q_ref,
    k_ref,
    v_ref,
    beta_ref,
    decay_ref,
    gate_ref,
    gain_ref,
    weight_ref,
    own_t,
    own_s,
    zin_t,
    zin_s,
    yin_t,
    yin_s,
    total_t,
    total_s,
    prefix_t,
    prefix_s,
    suffix,
    reach,
    sout,
    sin,
    within,
    qmap,
    gating,
    gated_ref,
    pair_out,
    pair_in,
    mine,
    chip_in,
    load,
    zsend_t,
    zsend_s,
    zrecv_t,
    zrecv_s,
    ysend_t,
    ysend_s,
    yrecv_t,
    yrecv_s,
    rsend,
    rrecv,
    psend,
    precv,
    csend,
    crecv,
):
    heads = v_ref.shape[1] // D
    kheads = k_ref.shape[1] // D
    group = heads // kheads
    chips = n // 2
    width = out_ref.shape[1]
    ctx, head = lax.axis_index("ctx"), lax.axis_index("head")
    y, z = ctx // nz, ctx % nz
    x, core = head // 2, head % 2
    sibling = x * 2 + 1 - core
    worker = z % 2 == core

    loads = [
        pltpu.make_async_copy(src, dst, load.at[i])
        for i, (src, dst) in enumerate(
            [
                (k_hbm, k_ref),
                (decay_hbm, decay_ref),
                (beta_hbm, beta_ref),
                (v_hbm, v_ref),
                (q_hbm, q_ref),
                (gate_hbm, gate_ref),
                (gain_hbm, gain_ref),
                (weight_hbm, weight_ref),
            ]
        )
    ]
    for copy in loads:
        copy.start()

    barrier = pltpu.get_barrier_semaphore()

    def greet(where):
        pl.semaphore_signal(barrier, inc=1, device_id=where, device_id_type=MESH)

    for dz in range(1, nz):
        greet((y * nz + (z + dz) % nz, head))
    for dy in range(1, ny):
        greet((((y + dy) % ny) * nz + z, head))
    greet((ctx, sibling))
    for dx in range(1, chips):
        greet((ctx, ((x + dx) % chips) * 2 + core))
    greeted = nz - 1 + ny - 1 + chips

    for copy in loads[:3]:
        copy.wait()

    row, col = iotas(D)
    causal, strict = row >= col, row > col
    eye = jnp.where(row == col, 1.0, 0.0).astype(F32)
    tri = jnp.where(causal, 1.0, 0.0).astype(F32)
    keys = jnp.stack([k_ref[:, i * D : (i + 1) * D] for i in range(kheads)])
    keys32 = keys.astype(F32)
    keys_t32 = jnp.stack([keys32[i].T for i in range(kheads)])
    keys_t = keys_t32.astype(BF16)
    r_col = lax.rsqrt(jnp.sum(keys32 * keys32, axis=2, keepdims=True) + 1e-06)
    r_row = lax.rsqrt(jnp.sum(keys_t32 * keys_t32, axis=1, keepdims=True) + 1e-06)
    gram = mm_bf16(keys, keys_t) * (r_col * r_row)

    beta_row = jax.nn.sigmoid(beta_ref[...])
    decay_row = decay_ref[...]
    cum_row = nt(decay_row, tri)
    cum_col = nt(tri, decay_row)
    beta_col = nt(eye, beta_row)
    exp_row = jnp.exp(cum_row)
    total = cum_row[:, D - 1 : D]
    exp_total = jnp.exp(total)
    tail_row = jnp.exp(total - cum_row)

    def per_head(fn):
        return jnp.stack([fn(h) for h in range(heads)])

    decay_mat = per_head(
        lambda h: jnp.exp(
            jnp.where(causal, cum_col[:, h : h + 1] - cum_row[h : h + 1, :], -1e30)
        )
    )
    strict_part = per_head(
        lambda h: jnp.where(
            strict, beta_col[:, h : h + 1] * gram[h // group] * decay_mat[h], 0.0
        )
    )
    inverse = unit_lower_inverse(strict_part)
    scaled = per_head(lambda h: inverse[h] * beta_row[h : h + 1, :])
    wy = mm_split(
        per_head(lambda h: scaled[h] * (exp_row[h : h + 1, :] * r_row[h // group])),
        per_head(lambda h: keys[h // group]),
    )
    tails = per_head(
        lambda h: keys_t32[h // group] * (r_row[h // group] * tail_row[h : h + 1, :])
    )
    moved = mm3(tails, wy)
    for h in range(heads):
        own_t[h] = exp_total[h : h + 1, :] * eye - moved[h]

    pl.semaphore_wait(barrier, greeted)

    def head_copy(k, own, zin, send, recv):
        h = (z // 2 + k) % heads
        return pltpu.make_async_remote_copy(
            src_ref=own.at[h],
            dst_ref=zin.at[z],
            send_sem=send.at[k],
            recv_sem=recv.at[z],
            device_id=(y * nz + 2 * h + core, head),
            device_id_type=MESH,
        )

    by_distance = sorted(range(heads), key=lambda k: -min(k, heads - k))
    move_t = (own_t, zin_t, zsend_t, zrecv_t)
    move_s = (own_s, zin_s, zsend_s, zrecv_s)

    def send_heads(move):
        for k in by_distance:
            if k:
                head_copy(k, *move).start()
            else:

                @pl.when(jnp.logical_not(worker))
                def _():
                    head_copy(0, *move).start()

                @pl.when(worker)
                def _():
                    move[1][pl.ds(z, 1)] = move[0][pl.ds(z // 2, 1)]

    send_heads(move_t)
    loads[3].wait()
    values = jnp.stack([v_ref[:, i * D : (i + 1) * D] for i in range(heads)])
    pseudo = mm_split(scaled, values)
    gained = mm3(tails, pseudo)
    for h in range(heads):
        own_s[h] = gained[h]
    send_heads(move_s)

    loads[4].wait()
    queries = jnp.stack([q_ref[:, i * D : (i + 1) * D] for i in range(kheads)])
    scores = mm_bf16(queries, keys_t) * r_row
    exp_col = jnp.exp(cum_col)
    wy_pseudo = jnp.concatenate([wy, pseudo], axis=2)
    mixed = mm3(per_head(lambda h: scores[h // group] * decay_mat[h]), wy_pseudo)
    for h in range(heads):
        within[h] = mixed[h, :, D:]
        qmap[h] = exp_col[:, h : h + 1] * queries[h // group].astype(F32) - mixed[h, :, :D]
    for copy in loads[5:]:
        copy.wait()
    for h in range(heads):
        gate = gate_ref[:, h * D : (h + 1) * D].astype(F32)
        gating[h] = gain_ref[...] * (gate / (1.0 + jnp.exp(-gate)))

    def row_copy(dy, src, yin, send, recv):
        return pltpu.make_async_remote_copy(
            src_ref=src,
            dst_ref=yin.at[dy],
            send_sem=send.at[dy],
            recv_sem=recv.at[dy],
            device_id=((y + dy) * nz + z, head),
            device_id_type=MESH,
        )

    far_rows = sorted(range(1, ny), key=lambda d: -min(d, ny - d))

    def each_row_t(act):
        for dy in far_rows:

            @pl.when((y > 0) & (y + dy < ny))
            def _():
                act(row_copy(dy, total_t, yin_t, ysend_t, yrecv_t))

    def each_row_s(act):
        for dy in far_rows:

            @pl.when(y + dy < ny)
            def _():
                act(row_copy(dy, total_s, yin_s, ysend_s, yrecv_s))

    def state_copy(dz):
        i = (z + dz) % nz
        return pltpu.make_async_remote_copy(
            src_ref=sout.at[i],
            dst_ref=sin.at[z // 2],
            send_sem=rsend.at[dz],
            recv_sem=rrecv.at[z // 2],
            device_id=(y * nz + i, head),
            device_id_type=MESH,
        )

    def arrived(dst, sem):
        pltpu.make_async_remote_copy(
            src_ref=dst,
            dst_ref=dst,
            send_sem=zsend_t.at[0],
            recv_sem=sem,
            device_id=(ctx, sibling),
            device_id_type=MESH,
        ).wait_recv()

    targets = sorted(range(nz), key=lambda d: -min(d, nz - d))

    @pl.when(worker)
    def _():
        def wait_place(zin, recv):
            for i in range(nz):

                @pl.when(z != i)
                def _():
                    arrived(zin.at[i], recv.at[i])

        wait_place(zin_t, zrecv_t)
        first = {(i, i + 1): zin_t[i] for i in range(nz)}

        def trans(low, high):
            if (low, high) not in first:
                span = 1 << ((high - low - 1).bit_length() - 1)
                middle = low + span if low % (2 * span) == 0 else high - span
                first[(low, high)] = mm3(trans(middle, high), trans(low, middle))
            return first[(low, high)]

        total_t[...] = trans(0, nz)
        each_row_t(lambda copy: copy.start())
        for i in range(1, nz):
            suffix[:, (i - 1) * D : i * D] = trans(i, nz)
        prefix_t[0] = eye
        for i in range(1, nz):
            prefix_t[i] = trans(0, i)

        wait_place(zin_s, zrecv_s)
        total_s[...] = zin_s[nz - 1] + mm3(
            suffix[...], zin_s[: nz - 1].reshape((nz - 1) * D, D)
        )
        each_row_s(lambda copy: copy.start())

        prefix_s[0] = jnp.zeros((D, D), F32)
        states = {(i, i + 1): zin_s[i] for i in range(nz)}

        def state_of(low, high):
            if (low, high) not in states:
                span = 1 << ((high - low - 1).bit_length() - 1)
                middle = low + span if low % (2 * span) == 0 else high - span
                states[(low, high)] = mm3(trans(middle, high), state_of(low, middle)) + state_of(
                    middle, high
                )
            return states[(low, high)]

        for i in range(1, nz):
            prefix_s[i] = state_of(0, i)

        reach[:, :D] = eye
        for dy in range(2, ny):
            here = slice((dy - 1) * D, dy * D)
            before = slice((dy - 2) * D, (dy - 1) * D)

            @pl.when(dy <= y)
            def _():
                arrived(yin_t.at[dy - 1], yrecv_t.at[dy - 1])
                if dy == 2:
                    reach[:, here] = yin_t[1]
                else:
                    reach[:, here] = mm3(reach[:, before], yin_t[dy - 1])

            @pl.when(dy > y)
            def _():
                reach[:, here] = jnp.zeros((D, D), F32)

        for dy in range(1, ny):

            @pl.when(dy <= y)
            def _():
                arrived(yin_s.at[dy], yrecv_s.at[dy])

            @pl.when(dy > y)
            def _():
                yin_s[dy] = jnp.zeros((D, D), F32)

        state = mm3(reach[...], yin_s[1:].reshape((ny - 1) * D, D))
        for dz in targets:
            i = (z + dz) % nz
            result = mm3(prefix_t[pl.ds(i, 1)][0], state) + prefix_s[pl.ds(i, 1)][0]
            if dz:
                sout[pl.ds(i, 1)] = result[None]
                state_copy(dz).start()
            else:
                sin[pl.ds(z // 2, 1)] = result[None]

    for h in range(heads):

        @pl.when(jnp.logical_not(worker) | (z // 2 != h))
        def _():
            arrived(sin.at[h], rrecv.at[h])

    core_out = within[...] + mm3(qmap[...], sin[...])
    scale = lax.rsqrt(jnp.mean(core_out * core_out, axis=2, keepdims=True) + 1e-06)
    for h in range(heads):
        gated_ref[:, h * D : (h + 1) * D] = (core_out[h] * scale[h] * gating[h]).astype(BF16)

    gated = gated_ref[...]

    def columns(chip, which):
        start = pl.multiple_of((chip * 2 + which) * width, width)
        return mm_bf16(gated, weight_ref[:, pl.ds(start, width)])

    def pair_copy(step):
        return pltpu.make_async_remote_copy(
            src_ref=pair_out.at[step],
            dst_ref=pair_in.at[step],
            send_sem=psend.at[step],
            recv_sem=precv.at[step],
            device_id=(ctx, sibling),
            device_id_type=MESH,
        )

    def chip_copy(step):
        return pltpu.make_async_remote_copy(
            src_ref=mine.at[step],
            dst_ref=chip_in.at[step],
            send_sem=csend.at[step],
            recv_sem=crecv.at[step],
            device_id=(ctx, ((x + step) % chips) * 2 + core),
            device_id_type=MESH,
        )

    order = sorted(range(chips), key=lambda s: -min(s, chips - s))
    for step in order:
        pair_out[step] = columns((x + step) % chips, 1 - core)
        pair_copy(step).start()
    for step in order:
        mine[step] = columns((x + step) % chips, core)
    for step in order:
        pair_copy(step).wait_recv()
        mine[step] = mine[step] + pair_in[step]
        if step:
            chip_copy(step).start()
    for move in (move_t, move_s):
        for k in range(heads):
            if k:
                head_copy(k, *move).wait_send()
            else:

                @pl.when(jnp.logical_not(worker))
                def _():
                    head_copy(0, *move).wait_send()

    @pl.when(worker)
    def _():
        each_row_t(lambda copy: copy.wait_send())
        each_row_s(lambda copy: copy.wait_send())
        for dz in targets:
            if dz:
                state_copy(dz).wait_send()

    for step in order:
        pair_copy(step).wait_send()

    summed = mine[0]
    for step in order[1:-1] + order[:-1][:1]:
        chip_copy(step).wait_recv()
        summed = summed + chip_in[step]
    out_ref[...] = summed.astype(BF16)

    for step in order:
        if step:
            chip_copy(step).wait_send()


def per_device(
    queries, key_rows, value_rows, beta_logit, log_decay, out_gate, norm_gain, out_weight
):
    heads = value_rows.shape[1] // D
    tokens = value_rows.shape[0]
    nz = 2 * heads
    ny = lax.axis_size("ctx") // nz
    n = lax.axis_size("head")
    width = out_weight.shape[1] // n
    vmem = pltpu.VMEM
    dma = pltpu.SemaphoreType.DMA
    args = (
        queries,
        key_rows,
        value_rows,
        beta_logit.T,
        log_decay.T,
        out_gate,
        norm_gain[None],
        out_weight,
    )
    return pl.pallas_call(
        functools.partial(kernel, ny, nz, n),
        out_shape=jax.ShapeDtypeStruct((tokens, width), BF16),
        in_specs=[pl.BlockSpec(memory_space=pltpu.HBM)] * len(args),
        out_specs=pl.BlockSpec(memory_space=vmem),
        scratch_shapes=[vmem(a.shape, a.dtype) for a in args]
        + [
            vmem((heads, D, D), F32),
            vmem((heads, D, D), F32),
            vmem((nz, D, D), F32),
            vmem((nz, D, D), F32),
            vmem((ny, D, D), F32),
            vmem((ny, D, D), F32),
            vmem((D, D), F32),
            vmem((D, D), F32),
            vmem((nz, D, D), F32),
            vmem((nz, D, D), F32),
            vmem((D, (nz - 1) * D), F32),
            vmem((D, (ny - 1) * D), F32),
            vmem((nz, D, D), F32),
            vmem((heads, D, D), F32),
            vmem((heads, D, D), F32),
            vmem((heads, D, D), F32),
            vmem((heads, D, D), F32),
            vmem((tokens, heads * D), BF16),
            vmem((n // 2, tokens, width), F32),
            vmem((n // 2, tokens, width), F32),
            vmem((n // 2, tokens, width), F32),
            vmem((n // 2, tokens, width), F32),
            dma((len(args),)),
            dma((heads,)),
            dma((heads,)),
            dma((nz,)),
            dma((nz,)),
            dma((ny,)),
            dma((ny,)),
            dma((ny,)),
            dma((ny,)),
            dma((nz,)),
            dma((heads,)),
            dma((n // 2,)),
            dma((n // 2,)),
            dma((n // 2,)),
            dma((n // 2,)),
        ],
        compiler_params=pltpu.CompilerParams(
            collective_id=0, has_side_effects=True, vmem_limit_bytes=56 * 2**20
        ),
        name="delta_layer",
    )(*args)


def solution(mesh):
    return jax.shard_map(
        per_device,
        mesh=mesh,
        in_specs=(
            P("ctx", "head"),
            P("ctx", "head"),
            P("ctx", "head"),
            P("ctx", "head"),
            P("ctx", "head"),
            P("ctx", "head"),
            P(),
            P("head", None),
        ),
        out_specs=P("ctx", "head"),
        check_vma=False,
    )
```

```python
import functools

import jax
import jax.numpy as jnp
from jax import lax
from jax.experimental import pallas as pl
from jax.experimental.pallas import tpu as pltpu
from jax.sharding import PartitionSpec as P

MESH = pl.DeviceIdType.MESH
F32 = jnp.float32
BF16 = jnp.bfloat16
D = 128
PARTS = 2
ROWS = D // PARTS


def mm(a, b):
    batch = tuple(range(a.ndim - 2))
    dims = (((a.ndim - 1,), (b.ndim - 2,)), (batch, batch))
    return lax.dot_general(a, b, dims, precision=lax.Precision.HIGHEST, preferred_element_type=F32)


def mm_bf16(a, b):
    batch = tuple(range(a.ndim - 2))
    dims = (((a.ndim - 1,), (b.ndim - 2,)), (batch, batch))
    return lax.dot_general(a, b, dims, preferred_element_type=F32)


def mm_split(a, b):
    high = a.astype(BF16)
    low = (a - high.astype(F32)).astype(BF16)
    return mm_bf16(high, b) + mm_bf16(low, b)


def cut(a):
    high = a.astype(BF16)
    return high, (a - high.astype(F32)).astype(BF16)


def mm3(a, b):
    a_high, a_low = cut(a)
    b_high, b_low = cut(b)
    return mm_bf16(a_high, b_high) + (mm_bf16(a_high, b_low) + mm_bf16(a_low, b_high))


def nt3(a, b_cut):
    batch = tuple(range(a.ndim - 2))
    dims = (((a.ndim - 1,), (a.ndim - 1,)), (batch, batch))

    def dot(left, right):
        return lax.dot_general(left, right, dims, preferred_element_type=F32)

    a_high, a_low = cut(a)
    b_high, b_low = b_cut
    return dot(a_high, b_high) + (dot(a_high, b_low) + dot(a_low, b_high))


def nt(a, b):
    return lax.dot_general(
        a, b, (((1,), (1,)), ((), ())), precision=lax.Precision.HIGHEST, preferred_element_type=F32
    )


def iotas(n):
    return (
        lax.broadcasted_iota(jnp.int32, (n, n), 0),
        lax.broadcasted_iota(jnp.int32, (n, n), 1),
    )


def unit_lower_inverse(strict_part):
    row, col = iotas(D)
    eye = jnp.where(row == col, 1.0, 0.0).astype(F32)

    def off(half):
        shift = half.bit_length() - 1
        rb, cb = row >> shift, col >> shift
        mask = ((rb ^ cb) == 1) & (rb > cb)
        return jnp.where(mask[None], strict_part, 0.0)

    inverse = eye[None] - off(1)
    half = 2
    while half < D:
        inverse = inverse - mm3(inverse, mm3(off(half), inverse))
        half *= 2
    return inverse


def kernel(
    ny,
    nz,
    n,
    q_hbm,
    k_hbm,
    v_hbm,
    beta_hbm,
    decay_hbm,
    gate_hbm,
    gain_hbm,
    weight_hbm,
    out_ref,
    q_ref,
    k_ref,
    v_ref,
    beta_ref,
    decay_ref,
    gate_ref,
    gain_ref,
    weight_ref,
    own_t,
    own_s,
    zin_t,
    zin_s,
    yin_t,
    yin_s,
    total_t,
    total_s,
    prefix_high,
    prefix_low,
    prefix_s,
    suffix,
    reach,
    sout,
    sin,
    within,
    qmap,
    gating,
    gated_ref,
    pair_out,
    pair_in,
    mine,
    chip_in,
    load,
    zsend_t,
    zsend_s,
    zrecv_t,
    zrecv_s,
    ysend_t,
    ysend_s,
    yrecv_t,
    yrecv_s,
    rsend,
    rrecv,
    psend,
    precv,
    csend,
    crecv,
):
    heads = v_ref.shape[1] // D
    kheads = k_ref.shape[1] // D
    group = heads // kheads
    chips = n // 2
    width = out_ref.shape[1]
    ctx, head = lax.axis_index("ctx"), lax.axis_index("head")
    y, z = ctx // nz, ctx % nz
    x, core = head // 2, head % 2
    sibling = x * 2 + 1 - core
    worker = z % 2 == core

    loads = [
        pltpu.make_async_copy(src, dst, load.at[i])
        for i, (src, dst) in enumerate(
            [
                (k_hbm, k_ref),
                (decay_hbm, decay_ref),
                (beta_hbm, beta_ref),
                (v_hbm, v_ref),
                (q_hbm, q_ref),
                (gate_hbm, gate_ref),
                (gain_hbm, gain_ref),
                (weight_hbm, weight_ref),
            ]
        )
    ]
    for copy in loads:
        copy.start()

    barrier = pltpu.get_barrier_semaphore()

    def greet(where):
        pl.semaphore_signal(barrier, inc=1, device_id=where, device_id_type=MESH)

    for dz in range(1, nz):
        greet((y * nz + (z + dz) % nz, head))
    for dy in range(1, ny):
        greet((((y + dy) % ny) * nz + z, head))
    greet((ctx, sibling))
    for dx in range(1, chips):
        greet((ctx, ((x + dx) % chips) * 2 + core))
    greeted = nz - 1 + ny - 1 + chips

    for copy in loads[:3]:
        copy.wait()

    row, col = iotas(D)
    causal, strict = row >= col, row > col
    eye = jnp.where(row == col, 1.0, 0.0).astype(F32)
    tri = jnp.where(causal, 1.0, 0.0).astype(F32)
    keys = jnp.stack([k_ref[:, i * D : (i + 1) * D] for i in range(kheads)])
    keys32 = keys.astype(F32)
    keys_t32 = jnp.stack([keys32[i].T for i in range(kheads)])
    keys_t = keys_t32.astype(BF16)
    r_col = lax.rsqrt(jnp.sum(keys32 * keys32, axis=2, keepdims=True) + 1e-06)
    r_row = lax.rsqrt(jnp.sum(keys_t32 * keys_t32, axis=1, keepdims=True) + 1e-06)
    gram = mm_bf16(keys, keys_t) * (r_col * r_row)

    beta_row = jax.nn.sigmoid(beta_ref[...])
    decay_row = decay_ref[...]
    cum_row = nt(decay_row, tri)
    cum_col = nt(tri, decay_row)
    beta_col = nt(eye, beta_row)
    exp_row = jnp.exp(cum_row)
    total = cum_row[:, D - 1 : D]
    exp_total = jnp.exp(total)
    tail_row = jnp.exp(total - cum_row)

    def per_head(fn):
        return jnp.stack([fn(h) for h in range(heads)])

    decay_mat = per_head(
        lambda h: jnp.exp(
            jnp.where(causal, cum_col[:, h : h + 1] - cum_row[h : h + 1, :], -1e30)
        )
    )
    strict_part = per_head(
        lambda h: jnp.where(
            strict, beta_col[:, h : h + 1] * gram[h // group] * decay_mat[h], 0.0
        )
    )
    inverse = unit_lower_inverse(strict_part)
    scaled = per_head(lambda h: inverse[h] * beta_row[h : h + 1, :])
    wy = mm_split(
        per_head(lambda h: scaled[h] * (exp_row[h : h + 1, :] * r_row[h // group])),
        per_head(lambda h: keys[h // group]),
    )
    tails = per_head(
        lambda h: keys_t32[h // group] * (r_row[h // group] * tail_row[h : h + 1, :])
    )
    moved = mm3(tails, wy)
    for h in range(heads):
        own_t[h] = exp_total[h : h + 1, :] * eye - moved[h]

    pl.semaphore_wait(barrier, greeted)

    def head_copy(k):
        h = (z // 2 + k) % heads
        return pltpu.make_async_remote_copy(
            src_ref=own_t.at[h],
            dst_ref=zin_t.at[z],
            send_sem=zsend_t.at[k],
            recv_sem=zrecv_t.at[z],
            device_id=(y * nz + 2 * h + core, head),
            device_id_type=MESH,
        )

    def part(p):
        return pl.ds(p * ROWS, ROWS)

    def head_part_copy(k, p):
        h = (z // 2 + k) % heads
        return pltpu.make_async_remote_copy(
            src_ref=own_s.at[h, part(p)],
            dst_ref=zin_s.at[z, part(p)],
            send_sem=zsend_s.at[p, k],
            recv_sem=zrecv_s.at[p, z],
            device_id=(y * nz + 2 * h + core, head),
            device_id_type=MESH,
        )

    def each_head_copy(act):
        for k in by_distance:
            if k:
                act(head_copy(k))
            else:

                @pl.when(jnp.logical_not(worker))
                def _():
                    act(head_copy(0))

    def each_head_part_copy(act):
        for p in range(PARTS):
            for k in by_distance:
                if k:
                    act(head_part_copy(k, p))
                else:

                    @pl.when(jnp.logical_not(worker))
                    def _():
                        act(head_part_copy(0, p))

    def keep_own(own, zin):
        @pl.when(worker)
        def _():
            zin[pl.ds(z, 1)] = own[pl.ds(z // 2, 1)]

    by_distance = sorted(range(heads), key=lambda k: -min(k, heads - k))
    each_head_copy(lambda copy: copy.start())
    keep_own(own_t, zin_t)
    loads[3].wait()
    values = jnp.stack([v_ref[:, i * D : (i + 1) * D] for i in range(heads)])
    pseudo = mm_split(scaled, values)
    gained = mm3(tails, pseudo)
    for h in range(heads):
        own_s[h] = gained[h].T
    each_head_part_copy(lambda copy: copy.start())
    keep_own(own_s, zin_s)

    loads[4].wait()
    queries = jnp.stack([q_ref[:, i * D : (i + 1) * D] for i in range(kheads)])
    scores = mm_bf16(queries, keys_t) * r_row
    exp_col = jnp.exp(cum_col)
    wy_pseudo = jnp.concatenate([wy, pseudo], axis=2)
    mixed = mm3(per_head(lambda h: scores[h // group] * decay_mat[h]), wy_pseudo)
    for h in range(heads):
        within[h] = mixed[h, :, D:]
        qmap[h] = exp_col[:, h : h + 1] * queries[h // group].astype(F32) - mixed[h, :, :D]
    for copy in loads[5:]:
        copy.wait()
    for h in range(heads):
        gate = gate_ref[:, h * D : (h + 1) * D].astype(F32)
        gating[h] = gain_ref[...] * (gate / (1.0 + jnp.exp(-gate)))

    def row_copy(dy):
        return pltpu.make_async_remote_copy(
            src_ref=total_t,
            dst_ref=yin_t.at[dy],
            send_sem=ysend_t.at[dy],
            recv_sem=yrecv_t.at[dy],
            device_id=((y + dy) * nz + z, head),
            device_id_type=MESH,
        )

    def row_part_copy(dy, p):
        return pltpu.make_async_remote_copy(
            src_ref=total_s.at[part(p)],
            dst_ref=yin_s.at[dy, part(p)],
            send_sem=ysend_s.at[p, dy],
            recv_sem=yrecv_s.at[p, dy],
            device_id=((y + dy) * nz + z, head),
            device_id_type=MESH,
        )

    far_rows = sorted(range(1, ny), key=lambda d: -min(d, ny - d))

    def each_row_t(act):
        for dy in far_rows:

            @pl.when((y > 0) & (y + dy < ny))
            def _():
                act(row_copy(dy))

    def each_row_s(act, p):
        for dy in far_rows:

            @pl.when(y + dy < ny)
            def _():
                act(row_part_copy(dy, p))

    def state_copy(dz, p):
        i = (z + dz) % nz
        return pltpu.make_async_remote_copy(
            src_ref=sout.at[i, part(p)],
            dst_ref=sin.at[z // 2, part(p)],
            send_sem=rsend.at[p, dz],
            recv_sem=rrecv.at[p, z // 2],
            device_id=(y * nz + i, head),
            device_id_type=MESH,
        )

    def arrived(dst, sem):
        pltpu.make_async_remote_copy(
            src_ref=dst,
            dst_ref=dst,
            send_sem=zsend_t.at[0],
            recv_sem=sem,
            device_id=(ctx, sibling),
            device_id_type=MESH,
        ).wait_recv()

    targets = sorted(range(nz), key=lambda d: -min(d, nz - d))

    @pl.when(worker)
    def _():
        for i in range(nz):

            @pl.when(z != i)
            def _():
                arrived(zin_t.at[i], zrecv_t.at[i])

        first = {(i, i + 1): zin_t[i] for i in range(nz)}

        def trans(low, high):
            if (low, high) not in first:
                span = 1 << ((high - low - 1).bit_length() - 1)
                middle = low + span if low % (2 * span) == 0 else high - span
                first[(low, high)] = mm3(trans(middle, high), trans(low, middle))
            return first[(low, high)]

        total_t[...] = trans(0, nz)
        each_row_t(lambda copy: copy.start())
        for i in range(1, nz):
            suffix[:, (i - 1) * D : i * D] = trans(i, nz)
        prefix_high[0] = eye.astype(BF16)
        prefix_low[0] = jnp.zeros((D, D), BF16)
        for i in range(1, nz):
            prefix_high[i], prefix_low[i] = cut(trans(0, i))

        suffix_cut = cut(suffix[...])
        for p in range(PARTS):
            for i in range(nz):

                @pl.when(z != i)
                def _():
                    arrived(zin_s.at[i, part(p)], zrecv_s.at[p, i])

            before = jnp.concatenate([zin_s[i, part(p)] for i in range(nz - 1)], axis=1)
            total_s[part(p)] = zin_s[nz - 1, part(p)] + nt3(before, suffix_cut)
            each_row_s(lambda copy: copy.start(), p)

        prefix_s[0] = jnp.zeros((D, D), F32)
        states = {(i, i + 1): zin_s[i] for i in range(nz)}

        def state_of(low, high):
            if (low, high) not in states:
                span = 1 << ((high - low - 1).bit_length() - 1)
                middle = low + span if low % (2 * span) == 0 else high - span
                states[(low, high)] = nt3(
                    state_of(low, middle), cut(trans(middle, high))
                ) + state_of(middle, high)
            return states[(low, high)]

        for i in range(1, nz):
            prefix_s[i] = state_of(0, i)

        for dy in range(1, ny):

            @pl.when(dy > y)
            def _():
                yin_s[dy] = jnp.zeros((D, D), F32)

            @pl.when(dy >= y)
            def _():
                yin_t[dy] = eye

            @pl.when(dy < y)
            def _():
                arrived(yin_t.at[dy], yrecv_t.at[dy])

        paths = {(dy, dy + 1): yin_t[dy] for dy in range(1, ny - 1)}

        def path(low, high):
            if (low, high) not in paths:
                span = 1 << ((high - low - 1).bit_length() - 1)
                paths[(low, high)] = mm3(path(low, low + span), path(low + span, high))
            return paths[(low, high)]

        reach[:, :D] = eye
        for dy in range(2, ny):
            reach[:, (dy - 1) * D : dy * D] = path(1, dy)
        reach_cut = cut(reach[...])
        for p in range(PARTS):
            for dy in range(1, ny):

                @pl.when(dy <= y)
                def _():
                    arrived(yin_s.at[dy, part(p)], yrecv_s.at[p, dy])

            rows_in = jnp.concatenate([yin_s[dy, part(p)] for dy in range(1, ny)], axis=1)
            state = nt3(rows_in, reach_cut)
            for dz in targets:
                i = (z + dz) % nz
                one = pl.ds(i, 1)
                result = (
                    nt3(state, (prefix_high[one][0], prefix_low[one][0]))
                    + prefix_s[one, part(p)][0]
                )
                if dz:
                    sout[one, part(p)] = result[None]
                    state_copy(dz, p).start()
                else:
                    sin[pl.ds(z // 2, 1), part(p)] = result[None]

    for h in range(heads):

        @pl.when(jnp.logical_not(worker) | (z // 2 != h))
        def _():
            for p in range(PARTS):
                arrived(sin.at[h, part(p)], rrecv.at[p, h])

    core_out = within[...] + nt3(qmap[...], cut(sin[...]))
    scale = lax.rsqrt(jnp.mean(core_out * core_out, axis=2, keepdims=True) + 1e-06)
    for h in range(heads):
        gated_ref[:, h * D : (h + 1) * D] = (core_out[h] * scale[h] * gating[h]).astype(BF16)

    gated = gated_ref[...]

    def columns(chip, which):
        start = pl.multiple_of((chip * 2 + which) * width, width)
        return mm_bf16(gated, weight_ref[:, pl.ds(start, width)])

    def pair_copy(step):
        return pltpu.make_async_remote_copy(
            src_ref=pair_out.at[step],
            dst_ref=pair_in.at[step],
            send_sem=psend.at[step],
            recv_sem=precv.at[step],
            device_id=(ctx, sibling),
            device_id_type=MESH,
        )

    def chip_copy(step):
        return pltpu.make_async_remote_copy(
            src_ref=mine.at[step],
            dst_ref=chip_in.at[step],
            send_sem=csend.at[step],
            recv_sem=crecv.at[step],
            device_id=(ctx, ((x + step) % chips) * 2 + core),
            device_id_type=MESH,
        )

    order = sorted(range(chips), key=lambda s: -min(s, chips - s))
    for step in order:
        pair_out[step] = columns((x + step) % chips, 1 - core)
        pair_copy(step).start()
    for step in order:
        mine[step] = columns((x + step) % chips, core)
    for step in order:
        pair_copy(step).wait_recv()
        mine[step] = mine[step] + pair_in[step]
        if step:
            chip_copy(step).start()
    each_head_copy(lambda copy: copy.wait_send())
    each_head_part_copy(lambda copy: copy.wait_send())

    @pl.when(worker)
    def _():
        each_row_t(lambda copy: copy.wait_send())
        for p in range(PARTS):
            each_row_s(lambda copy: copy.wait_send(), p)
            for dz in targets:
                if dz:
                    state_copy(dz, p).wait_send()

    for step in order:
        pair_copy(step).wait_send()

    summed = mine[0]
    for step in order[1:-1] + order[:-1][:1]:
        chip_copy(step).wait_recv()
        summed = summed + chip_in[step]
    out_ref[...] = summed.astype(BF16)

    for step in order:
        if step:
            chip_copy(step).wait_send()


def per_device(
    queries, key_rows, value_rows, beta_logit, log_decay, out_gate, norm_gain, out_weight
):
    heads = value_rows.shape[1] // D
    tokens = value_rows.shape[0]
    nz = 2 * heads
    ny = lax.axis_size("ctx") // nz
    n = lax.axis_size("head")
    width = out_weight.shape[1] // n
    vmem = pltpu.VMEM
    dma = pltpu.SemaphoreType.DMA
    args = (
        queries,
        key_rows,
        value_rows,
        beta_logit.T,
        log_decay.T,
        out_gate,
        norm_gain[None],
        out_weight,
    )
    return pl.pallas_call(
        functools.partial(kernel, ny, nz, n),
        out_shape=jax.ShapeDtypeStruct((tokens, width), BF16),
        in_specs=[pl.BlockSpec(memory_space=pltpu.HBM)] * len(args),
        out_specs=pl.BlockSpec(memory_space=vmem),
        scratch_shapes=[vmem(a.shape, a.dtype) for a in args]
        + [
            vmem((heads, D, D), F32),
            vmem((heads, D, D), F32),
            vmem((nz, D, D), F32),
            vmem((nz, D, D), F32),
            vmem((ny, D, D), F32),
            vmem((ny, D, D), F32),
            vmem((D, D), F32),
            vmem((D, D), F32),
            vmem((nz, D, D), BF16),
            vmem((nz, D, D), BF16),
            vmem((nz, D, D), F32),
            vmem((D, (nz - 1) * D), F32),
            vmem((D, (ny - 1) * D), F32),
            vmem((nz, D, D), F32),
            vmem((heads, D, D), F32),
            vmem((heads, D, D), F32),
            vmem((heads, D, D), F32),
            vmem((heads, D, D), F32),
            vmem((tokens, heads * D), BF16),
            vmem((n // 2, tokens, width), F32),
            vmem((n // 2, tokens, width), F32),
            vmem((n // 2, tokens, width), F32),
            vmem((n // 2, tokens, width), F32),
            dma((len(args),)),
            dma((heads,)),
            dma((PARTS, heads)),
            dma((nz,)),
            dma((PARTS, nz)),
            dma((ny,)),
            dma((PARTS, ny)),
            dma((ny,)),
            dma((PARTS, ny)),
            dma((PARTS, nz)),
            dma((PARTS, heads)),
            dma((n // 2,)),
            dma((n // 2,)),
            dma((n // 2,)),
            dma((n // 2,)),
        ],
        compiler_params=pltpu.CompilerParams(
            collective_id=0, has_side_effects=True, vmem_limit_bytes=56 * 2**20
        ),
        name="delta_layer",
    )(*args)


def solution(mesh):
    return jax.shard_map(
        per_device,
        mesh=mesh,
        in_specs=(
            P("ctx", "head"),
            P("ctx", "head"),
            P("ctx", "head"),
            P("ctx", "head"),
            P("ctx", "head"),
            P("ctx", "head"),
            P(),
            P("head", None),
        ),
        out_specs=P("ctx", "head"),
        check_vma=False,
    )
```

```python
import functools

import jax
import jax.numpy as jnp
from jax import lax
from jax.experimental import pallas as pl
from jax.experimental.pallas import tpu as pltpu
from jax.sharding import PartitionSpec as P

MESH = pl.DeviceIdType.MESH
F32 = jnp.float32
BF16 = jnp.bfloat16
D = 128
PARTS = 2
ROWS = D // PARTS


def mm(a, b):
    batch = tuple(range(a.ndim - 2))
    dims = (((a.ndim - 1,), (b.ndim - 2,)), (batch, batch))
    return lax.dot_general(a, b, dims, precision=lax.Precision.HIGHEST, preferred_element_type=F32)


def mm_bf16(a, b):
    batch = tuple(range(a.ndim - 2))
    dims = (((a.ndim - 1,), (b.ndim - 2,)), (batch, batch))
    return lax.dot_general(a, b, dims, preferred_element_type=F32)


def mm_split(a, b):
    high = a.astype(BF16)
    low = (a - high.astype(F32)).astype(BF16)
    return mm_bf16(high, b) + mm_bf16(low, b)


def cut(a):
    high = a.astype(BF16)
    return high, (a - high.astype(F32)).astype(BF16)


def mm3(a, b):
    a_high, a_low = cut(a)
    b_high, b_low = cut(b)
    return mm_bf16(a_high, b_high) + (mm_bf16(a_high, b_low) + mm_bf16(a_low, b_high))


def nt3(a, b_cut):
    batch = tuple(range(a.ndim - 2))
    dims = (((a.ndim - 1,), (a.ndim - 1,)), (batch, batch))

    def dot(left, right):
        return lax.dot_general(left, right, dims, preferred_element_type=F32)

    a_high, a_low = cut(a)
    b_high, b_low = b_cut
    return dot(a_high, b_high) + (dot(a_high, b_low) + dot(a_low, b_high))


def nt(a, b):
    return lax.dot_general(
        a, b, (((1,), (1,)), ((), ())), precision=lax.Precision.HIGHEST, preferred_element_type=F32
    )


def iotas(n):
    return (
        lax.broadcasted_iota(jnp.int32, (n, n), 0),
        lax.broadcasted_iota(jnp.int32, (n, n), 1),
    )


def unit_lower_inverse(strict_part):
    row, col = iotas(D)
    eye = jnp.where(row == col, 1.0, 0.0).astype(F32)

    def off(half):
        shift = half.bit_length() - 1
        rb, cb = row >> shift, col >> shift
        mask = ((rb ^ cb) == 1) & (rb > cb)
        return jnp.where(mask[None], strict_part, 0.0)

    inverse = eye[None] - off(1)
    half = 2
    while half < D:
        inverse = inverse - mm3(inverse, mm3(off(half), inverse))
        half *= 2
    return inverse


def kernel(
    ny,
    nz,
    n,
    q_hbm,
    k_hbm,
    v_hbm,
    beta_hbm,
    decay_hbm,
    gate_hbm,
    gain_hbm,
    weight_hbm,
    out_ref,
    q_ref,
    k_ref,
    v_ref,
    beta_ref,
    decay_ref,
    gate_ref,
    gain_ref,
    weight_ref,
    own_t,
    own_s,
    zin_t,
    zin_s,
    yin_t,
    yin_s,
    total_t,
    total_s,
    prefix_high,
    prefix_low,
    prefix_s,
    suffix,
    reach,
    sout,
    sin,
    within,
    qmap,
    gating,
    gated_ref,
    pair_out,
    pair_in,
    mine,
    chip_in,
    ready,
    load,
    zsend_t,
    zsend_s,
    zrecv_t,
    zrecv_s,
    ysend_t,
    ysend_s,
    yrecv_t,
    yrecv_s,
    rsend,
    rrecv,
    psend,
    precv,
    csend,
    crecv,
):
    heads = v_ref.shape[1] // D
    kheads = k_ref.shape[1] // D
    group = heads // kheads
    chips = n // 2
    width = out_ref.shape[1]
    ctx, head = lax.axis_index("ctx"), lax.axis_index("head")
    y, z = ctx // nz, ctx % nz
    x, core = head // 2, head % 2
    sibling = x * 2 + 1 - core
    worker = z % 2 == core

    loads = [
        pltpu.make_async_copy(src, dst, load.at[i])
        for i, (src, dst) in enumerate(
            [
                (k_hbm, k_ref),
                (decay_hbm, decay_ref),
                (beta_hbm, beta_ref),
                (v_hbm, v_ref),
                (q_hbm, q_ref),
                (gate_hbm, gate_ref),
                (gain_hbm, gain_ref),
                (weight_hbm, weight_ref),
            ]
        )
    ]
    for copy in loads:
        copy.start()

    barrier = pltpu.get_barrier_semaphore()

    def greet(where):
        pl.semaphore_signal(barrier, inc=1, device_id=where, device_id_type=MESH)

    for other in range(1, nz):

        @pl.when(other > z)
        def _():
            greet((y * nz + other, head))

    for other in range(ny - 1):

        @pl.when(other < y)
        def _():
            greet((other * nz + z, head))

    greet((ctx, sibling))
    for dx in range(1, chips):
        greet((ctx, ((x + dx) % chips) * 2 + core))

    for copy in loads[:3]:
        copy.wait()

    row, col = iotas(D)
    causal, strict = row >= col, row > col
    eye = jnp.where(row == col, 1.0, 0.0).astype(F32)
    tri = jnp.where(causal, 1.0, 0.0).astype(F32)
    keys = jnp.stack([k_ref[:, i * D : (i + 1) * D] for i in range(kheads)])
    keys32 = keys.astype(F32)
    keys_t32 = jnp.stack([keys32[i].T for i in range(kheads)])
    keys_t = keys_t32.astype(BF16)
    r_col = lax.rsqrt(jnp.sum(keys32 * keys32, axis=2, keepdims=True) + 1e-06)
    r_row = lax.rsqrt(jnp.sum(keys_t32 * keys_t32, axis=1, keepdims=True) + 1e-06)
    gram = mm_bf16(keys, keys_t) * (r_col * r_row)

    beta_row = jax.nn.sigmoid(beta_ref[...])
    decay_row = decay_ref[...]
    cum_row = nt(decay_row, tri)
    cum_col = nt(tri, decay_row)
    beta_col = nt(eye, beta_row)
    exp_row = jnp.exp(cum_row)
    total = cum_row[:, D - 1 : D]
    exp_total = jnp.exp(total)
    tail_row = jnp.exp(total - cum_row)

    def per_head(fn):
        return jnp.stack([fn(h) for h in range(heads)])

    decay_mat = per_head(
        lambda h: jnp.exp(
            jnp.where(causal, cum_col[:, h : h + 1] - cum_row[h : h + 1, :], -1e30)
        )
    )
    strict_part = per_head(
        lambda h: jnp.where(
            strict, beta_col[:, h : h + 1] * gram[h // group] * decay_mat[h], 0.0
        )
    )
    pl.semaphore_wait(barrier, z + (ny - 1 - y) + chips)
    for other in range(nz - 1):

        @pl.when(other < z)
        def _():
            pl.semaphore_signal(
                ready.at[z], inc=1, device_id=(y * nz + other, head), device_id_type=MESH
            )

    inverse = unit_lower_inverse(strict_part)
    scaled = per_head(lambda h: inverse[h] * beta_row[h : h + 1, :])
    wy = mm_split(
        per_head(lambda h: scaled[h] * (exp_row[h : h + 1, :] * r_row[h // group])),
        per_head(lambda h: keys[h // group]),
    )
    tails = per_head(
        lambda h: keys_t32[h // group] * (r_row[h // group] * tail_row[h : h + 1, :])
    )
    moved = mm3(tails, wy)
    for h in range(heads):
        own_t[h] = exp_total[h : h + 1, :] * eye - moved[h]

    def head_copy(h):
        return pltpu.make_async_remote_copy(
            src_ref=own_t.at[h],
            dst_ref=zin_t.at[z],
            send_sem=zsend_t.at[h],
            recv_sem=zrecv_t.at[z],
            device_id=(y * nz + 2 * h + core, head),
            device_id_type=MESH,
        )

    def part(p):
        return pl.ds(p * ROWS, ROWS)

    def head_part_copy(k, p):
        h = (z // 2 + k) % heads
        return pltpu.make_async_remote_copy(
            src_ref=own_s.at[h, part(p)],
            dst_ref=zin_s.at[z, part(p)],
            send_sem=zsend_s.at[p, k],
            recv_sem=zrecv_s.at[p, z],
            device_id=(y * nz + 2 * h + core, head),
            device_id_type=MESH,
        )

    by_distance = sorted(range(heads), key=lambda k: -min(k, heads - k))

    def each_head_copy(act, before=lambda h: None):
        for h in range(heads):
            before(h)

            @pl.when(z != 2 * h + core)
            def _():
                act(head_copy(h))

    def each_head_part_copy(act):
        for p in range(PARTS):
            for k in by_distance:
                if k:
                    act(head_part_copy(k, p))
                else:

                    @pl.when(jnp.logical_not(worker))
                    def _():
                        act(head_part_copy(0, p))

    def await_ready(h):
        for other in (2 * h, 2 * h + 1):

            @pl.when(other > z)
            def _():
                pl.semaphore_wait(ready.at[other], 1)

    def keep_own(own, zin):
        @pl.when(worker)
        def _():
            zin[pl.ds(z, 1)] = own[pl.ds(z // 2, 1)]

    each_head_copy(lambda copy: copy.start(), await_ready)
    keep_own(own_t, zin_t)
    loads[3].wait()
    values = jnp.stack([v_ref[:, i * D : (i + 1) * D] for i in range(heads)])
    pseudo = mm_split(scaled, values)
    gained = mm3(tails, pseudo)
    for h in range(heads):
        own_s[h] = gained[h].T
    each_head_part_copy(lambda copy: copy.start())
    keep_own(own_s, zin_s)

    loads[4].wait()
    queries = jnp.stack([q_ref[:, i * D : (i + 1) * D] for i in range(kheads)])
    scores = mm_bf16(queries, keys_t) * r_row
    exp_col = jnp.exp(cum_col)
    wy_pseudo = jnp.concatenate([wy, pseudo], axis=2)
    mixed = mm3(per_head(lambda h: scores[h // group] * decay_mat[h]), wy_pseudo)
    for h in range(heads):
        within[h] = mixed[h, :, D:]
        qmap[h] = exp_col[:, h : h + 1] * queries[h // group].astype(F32) - mixed[h, :, :D]
    for copy in loads[5:]:
        copy.wait()
    for h in range(heads):
        gate = gate_ref[:, h * D : (h + 1) * D].astype(F32)
        gating[h] = gain_ref[...] * (gate / (1.0 + jnp.exp(-gate)))

    def row_copy(dy):
        return pltpu.make_async_remote_copy(
            src_ref=total_t,
            dst_ref=yin_t.at[dy],
            send_sem=ysend_t.at[dy],
            recv_sem=yrecv_t.at[dy],
            device_id=((y + dy) * nz + z, head),
            device_id_type=MESH,
        )

    def row_part_copy(dy, p):
        return pltpu.make_async_remote_copy(
            src_ref=total_s.at[part(p)],
            dst_ref=yin_s.at[dy, part(p)],
            send_sem=ysend_s.at[p, dy],
            recv_sem=yrecv_s.at[p, dy],
            device_id=((y + dy) * nz + z, head),
            device_id_type=MESH,
        )

    far_rows = sorted(range(1, ny), key=lambda d: -min(d, ny - d))

    def each_row_t(act):
        for dy in far_rows:

            @pl.when((y > 0) & (y + dy < ny))
            def _():
                act(row_copy(dy))

    def each_row_s(act, p):
        for dy in far_rows:

            @pl.when(y + dy < ny)
            def _():
                act(row_part_copy(dy, p))

    def state_copy(dz, p):
        i = (z + dz) % nz
        return pltpu.make_async_remote_copy(
            src_ref=sout.at[i, part(p)],
            dst_ref=sin.at[z // 2, part(p)],
            send_sem=rsend.at[p, dz],
            recv_sem=rrecv.at[p, z // 2],
            device_id=(y * nz + i, head),
            device_id_type=MESH,
        )

    def arrived(dst, sem):
        pltpu.make_async_remote_copy(
            src_ref=dst,
            dst_ref=dst,
            send_sem=zsend_t.at[0],
            recv_sem=sem,
            device_id=(ctx, sibling),
            device_id_type=MESH,
        ).wait_recv()

    targets = sorted(range(nz), key=lambda d: -min(d, nz - d))

    @pl.when(worker)
    def _():
        for i in range(nz):

            @pl.when(z != i)
            def _():
                arrived(zin_t.at[i], zrecv_t.at[i])

        first = {(i, i + 1): zin_t[i] for i in range(nz)}

        def trans(low, high):
            if (low, high) not in first:
                span = 1 << ((high - low - 1).bit_length() - 1)
                middle = low + span if low % (2 * span) == 0 else high - span
                first[(low, high)] = mm3(trans(middle, high), trans(low, middle))
            return first[(low, high)]

        total_t[...] = trans(0, nz)
        each_row_t(lambda copy: copy.start())
        for i in range(1, nz):
            suffix[:, (i - 1) * D : i * D] = trans(i, nz)
        prefix_high[0] = eye.astype(BF16)
        prefix_low[0] = jnp.zeros((D, D), BF16)
        for i in range(1, nz):
            prefix_high[i], prefix_low[i] = cut(trans(0, i))

        suffix_cut = cut(suffix[...])
        for p in range(PARTS):
            for i in range(nz):

                @pl.when(z != i)
                def _():
                    arrived(zin_s.at[i, part(p)], zrecv_s.at[p, i])

            before = jnp.concatenate([zin_s[i, part(p)] for i in range(nz - 1)], axis=1)
            total_s[part(p)] = zin_s[nz - 1, part(p)] + nt3(before, suffix_cut)
            each_row_s(lambda copy: copy.start(), p)

        prefix_s[0] = jnp.zeros((D, D), F32)
        states = {(i, i + 1): zin_s[i] for i in range(nz)}

        def state_of(low, high):
            if (low, high) not in states:
                span = 1 << ((high - low - 1).bit_length() - 1)
                middle = low + span if low % (2 * span) == 0 else high - span
                states[(low, high)] = nt3(
                    state_of(low, middle), cut(trans(middle, high))
                ) + state_of(middle, high)
            return states[(low, high)]

        for i in range(1, nz):
            prefix_s[i] = state_of(0, i)

        for dy in range(1, ny):

            @pl.when(dy > y)
            def _():
                yin_s[dy] = jnp.zeros((D, D), F32)

            @pl.when(dy >= y)
            def _():
                yin_t[dy] = eye

            @pl.when(dy < y)
            def _():
                arrived(yin_t.at[dy], yrecv_t.at[dy])

        paths = {(dy, dy + 1): yin_t[dy] for dy in range(1, ny - 1)}

        def path(low, high):
            if (low, high) not in paths:
                span = 1 << ((high - low - 1).bit_length() - 1)
                paths[(low, high)] = mm3(path(low, low + span), path(low + span, high))
            return paths[(low, high)]

        reach[:, :D] = eye
        for dy in range(2, ny):
            reach[:, (dy - 1) * D : dy * D] = path(1, dy)
        reach_cut = cut(reach[...])
        for p in range(PARTS):
            for dy in range(1, ny):

                @pl.when(dy <= y)
                def _():
                    arrived(yin_s.at[dy, part(p)], yrecv_s.at[p, dy])

            rows_in = jnp.concatenate([yin_s[dy, part(p)] for dy in range(1, ny)], axis=1)
            state = nt3(rows_in, reach_cut)
            for dz in targets:
                i = (z + dz) % nz
                one = pl.ds(i, 1)
                result = (
                    nt3(state, (prefix_high[one][0], prefix_low[one][0]))
                    + prefix_s[one, part(p)][0]
                )
                if dz:
                    sout[one, part(p)] = result[None]
                    state_copy(dz, p).start()
                else:
                    sin[pl.ds(z // 2, 1), part(p)] = result[None]

    for h in range(heads):

        @pl.when(jnp.logical_not(worker) | (z // 2 != h))
        def _():
            for p in range(PARTS):
                arrived(sin.at[h, part(p)], rrecv.at[p, h])

    core_out = within[...] + nt3(qmap[...], cut(sin[...]))
    scale = lax.rsqrt(jnp.mean(core_out * core_out, axis=2, keepdims=True) + 1e-06)
    for h in range(heads):
        gated_ref[:, h * D : (h + 1) * D] = (core_out[h] * scale[h] * gating[h]).astype(BF16)

    gated = gated_ref[...]

    def columns(chip, which):
        start = pl.multiple_of((chip * 2 + which) * width, width)
        return mm_bf16(gated, weight_ref[:, pl.ds(start, width)])

    def pair_copy(step):
        return pltpu.make_async_remote_copy(
            src_ref=pair_out.at[step],
            dst_ref=pair_in.at[step],
            send_sem=psend.at[step],
            recv_sem=precv.at[step],
            device_id=(ctx, sibling),
            device_id_type=MESH,
        )

    def chip_copy(step):
        return pltpu.make_async_remote_copy(
            src_ref=mine.at[step],
            dst_ref=chip_in.at[step],
            send_sem=csend.at[step],
            recv_sem=crecv.at[step],
            device_id=(ctx, ((x + step) % chips) * 2 + core),
            device_id_type=MESH,
        )

    order = sorted(range(chips), key=lambda s: -min(s, chips - s))
    for step in order:
        pair_out[step] = columns((x + step) % chips, 1 - core)
        pair_copy(step).start()
    for step in order:
        mine[step] = columns((x + step) % chips, core)
    for step in order:
        pair_copy(step).wait_recv()
        mine[step] = mine[step] + pair_in[step]
        if step:
            chip_copy(step).start()
    each_head_copy(lambda copy: copy.wait_send())
    each_head_part_copy(lambda copy: copy.wait_send())

    @pl.when(worker)
    def _():
        each_row_t(lambda copy: copy.wait_send())
        for p in range(PARTS):
            each_row_s(lambda copy: copy.wait_send(), p)
            for dz in targets:
                if dz:
                    state_copy(dz, p).wait_send()

    for step in order:
        pair_copy(step).wait_send()

    summed = mine[0]
    for step in order[1:-1] + order[:-1][:1]:
        chip_copy(step).wait_recv()
        summed = summed + chip_in[step]
    out_ref[...] = summed.astype(BF16)

    for step in order:
        if step:
            chip_copy(step).wait_send()


def per_device(
    queries, key_rows, value_rows, beta_logit, log_decay, out_gate, norm_gain, out_weight
):
    heads = value_rows.shape[1] // D
    tokens = value_rows.shape[0]
    nz = 2 * heads
    ny = lax.axis_size("ctx") // nz
    n = lax.axis_size("head")
    width = out_weight.shape[1] // n
    vmem = pltpu.VMEM
    dma = pltpu.SemaphoreType.DMA
    args = (
        queries,
        key_rows,
        value_rows,
        beta_logit.T,
        log_decay.T,
        out_gate,
        norm_gain[None],
        out_weight,
    )
    return pl.pallas_call(
        functools.partial(kernel, ny, nz, n),
        out_shape=vmem((tokens, width), BF16),
        in_specs=[pl.BlockSpec(memory_space=pltpu.HBM)] * len(args),
        out_specs=pl.BlockSpec(memory_space=vmem),
        scratch_shapes=[vmem(a.shape, a.dtype) for a in args]
        + [
            vmem((heads, D, D), F32),
            vmem((heads, D, D), F32),
            vmem((nz, D, D), F32),
            vmem((nz, D, D), F32),
            vmem((ny, D, D), F32),
            vmem((ny, D, D), F32),
            vmem((D, D), F32),
            vmem((D, D), F32),
            vmem((nz, D, D), BF16),
            vmem((nz, D, D), BF16),
            vmem((nz, D, D), F32),
            vmem((D, (nz - 1) * D), F32),
            vmem((D, (ny - 1) * D), F32),
            vmem((nz, D, D), F32),
            vmem((heads, D, D), F32),
            vmem((heads, D, D), F32),
            vmem((heads, D, D), F32),
            vmem((heads, D, D), F32),
            vmem((tokens, heads * D), BF16),
            vmem((n // 2, tokens, width), F32),
            vmem((n // 2, tokens, width), F32),
            vmem((n // 2, tokens, width), F32),
            vmem((n // 2, tokens, width), F32),
            pltpu.SemaphoreType.REGULAR((nz,)),
            dma((len(args),)),
            dma((heads,)),
            dma((PARTS, heads)),
            dma((nz,)),
            dma((PARTS, nz)),
            dma((ny,)),
            dma((PARTS, ny)),
            dma((ny,)),
            dma((PARTS, ny)),
            dma((PARTS, nz)),
            dma((PARTS, heads)),
            dma((n // 2,)),
            dma((n // 2,)),
            dma((n // 2,)),
            dma((n // 2,)),
        ],
        compiler_params=pltpu.CompilerParams(
            collective_id=0, has_side_effects=True, vmem_limit_bytes=56 * 2**20
        ),
        name="delta_layer",
    )(*args)


def solution(mesh):
    return jax.shard_map(
        per_device,
        mesh=mesh,
        in_specs=(
            P("ctx", "head"),
            P("ctx", "head"),
            P("ctx", "head"),
            P("ctx", "head"),
            P("ctx", "head"),
            P("ctx", "head"),
            P(),
            P("head", None),
        ),
        out_specs=P("ctx", "head"),
        check_vma=False,
    )
```

```python
import functools

import jax
import jax.numpy as jnp
from jax import lax
from jax.experimental import pallas as pl
from jax.experimental.pallas import tpu as pltpu
from jax.sharding import PartitionSpec as P

MESH = pl.DeviceIdType.MESH
F32 = jnp.float32
BF16 = jnp.bfloat16
D = 128
PARTS = 2
ROWS = D // PARTS


def mm(a, b):
    batch = tuple(range(a.ndim - 2))
    dims = (((a.ndim - 1,), (b.ndim - 2,)), (batch, batch))
    return lax.dot_general(a, b, dims, precision=lax.Precision.HIGHEST, preferred_element_type=F32)


def mm_bf16(a, b):
    batch = tuple(range(a.ndim - 2))
    dims = (((a.ndim - 1,), (b.ndim - 2,)), (batch, batch))
    return lax.dot_general(a, b, dims, preferred_element_type=F32)


def mm_split(a, b):
    high = a.astype(BF16)
    low = (a - high.astype(F32)).astype(BF16)
    return mm_bf16(high, b) + mm_bf16(low, b)


def cut(a):
    high = a.astype(BF16)
    return high, (a - high.astype(F32)).astype(BF16)


def mm3(a, b):
    a_high, a_low = cut(a)
    b_high, b_low = cut(b)
    return mm_bf16(a_high, b_high) + (mm_bf16(a_high, b_low) + mm_bf16(a_low, b_high))


def nt3(a, b_cut):
    batch = tuple(range(a.ndim - 2))
    dims = (((a.ndim - 1,), (a.ndim - 1,)), (batch, batch))

    def dot(left, right):
        return lax.dot_general(left, right, dims, preferred_element_type=F32)

    a_high, a_low = cut(a)
    b_high, b_low = b_cut
    return dot(a_high, b_high) + (dot(a_high, b_low) + dot(a_low, b_high))


def nt(a, b):
    return lax.dot_general(
        a, b, (((1,), (1,)), ((), ())), precision=lax.Precision.HIGHEST, preferred_element_type=F32
    )


def iotas(n):
    return (
        lax.broadcasted_iota(jnp.int32, (n, n), 0),
        lax.broadcasted_iota(jnp.int32, (n, n), 1),
    )


def unit_lower_inverse(strict_part):
    row, col = iotas(D)
    eye = jnp.where(row == col, 1.0, 0.0).astype(F32)

    def off(half):
        shift = half.bit_length() - 1
        rb, cb = row >> shift, col >> shift
        mask = ((rb ^ cb) == 1) & (rb > cb)
        return jnp.where(mask[None], strict_part, 0.0)

    inverse = eye[None] - off(1)
    half = 2
    while half < D:
        inverse = inverse - mm3(inverse, mm3(off(half), inverse))
        half *= 2
    return inverse


def kernel(
    ny,
    nz,
    n,
    q_hbm,
    k_hbm,
    v_hbm,
    beta_hbm,
    decay_hbm,
    gate_hbm,
    gain_hbm,
    weight_hbm,
    out_ref,
    q_ref,
    k_ref,
    v_ref,
    beta_ref,
    decay_ref,
    gate_ref,
    gain_ref,
    weight_ref,
    own_t,
    own_s,
    zin_t,
    zin_s,
    yin_t,
    yin_s,
    total_t,
    total_s,
    prefix_high,
    prefix_low,
    prefix_s,
    suffix,
    reach,
    sout,
    sin,
    within,
    qmap,
    gating,
    gated_ref,
    pair_out,
    pair_in,
    mine,
    chip_in,
    load,
    zsend_t,
    zsend_s,
    zrecv_t,
    zrecv_s,
    ysend_t,
    ysend_s,
    yrecv_t,
    yrecv_s,
    rsend,
    rrecv,
    psend,
    precv,
    csend,
    crecv,
):
    heads = v_ref.shape[1] // D
    kheads = k_ref.shape[1] // D
    group = heads // kheads
    chips = n // 2
    width = out_ref.shape[1]
    ctx, head = lax.axis_index("ctx"), lax.axis_index("head")
    y, z = ctx // nz, ctx % nz
    x, core = head // 2, head % 2
    sibling = x * 2 + 1 - core
    worker = z % 2 == core

    loads = [
        pltpu.make_async_copy(src, dst, load.at[i])
        for i, (src, dst) in enumerate(
            [
                (k_hbm, k_ref),
                (decay_hbm, decay_ref),
                (beta_hbm, beta_ref),
                (v_hbm, v_ref),
                (q_hbm, q_ref),
                (gate_hbm, gate_ref),
                (gain_hbm, gain_ref),
                (weight_hbm, weight_ref),
            ]
        )
    ]
    for copy in loads:
        copy.start()

    barrier = pltpu.get_barrier_semaphore()

    def greet(where):
        pl.semaphore_signal(barrier, inc=1, device_id=where, device_id_type=MESH)

    for dz in range(1, nz):
        greet((y * nz + (z + dz) % nz, head))
    for dy in range(1, ny):
        greet((((y + dy) % ny) * nz + z, head))
    greet((ctx, sibling))
    for dx in range(1, chips):
        greet((ctx, ((x + dx) % chips) * 2 + core))
    greeted = nz - 1 + ny - 1 + chips

    for copy in loads[:3]:
        copy.wait()

    row, col = iotas(D)
    causal, strict = row >= col, row > col
    eye = jnp.where(row == col, 1.0, 0.0).astype(F32)
    tri = jnp.where(causal, 1.0, 0.0).astype(F32)
    keys = jnp.stack([k_ref[:, i * D : (i + 1) * D] for i in range(kheads)])
    keys32 = keys.astype(F32)
    keys_t32 = jnp.stack([keys32[i].T for i in range(kheads)])
    keys_t = keys_t32.astype(BF16)
    r_col = lax.rsqrt(jnp.sum(keys32 * keys32, axis=2, keepdims=True) + 1e-06)
    r_row = lax.rsqrt(jnp.sum(keys_t32 * keys_t32, axis=1, keepdims=True) + 1e-06)
    gram = mm_bf16(keys, keys_t) * (r_col * r_row)

    beta_row = jax.nn.sigmoid(beta_ref[...])
    decay_row = decay_ref[...]
    cum_row = nt(decay_row, tri)
    cum_col = nt(tri, decay_row)
    beta_col = nt(eye, beta_row)
    exp_row = jnp.exp(cum_row)
    total = cum_row[:, D - 1 : D]
    exp_total = jnp.exp(total)
    tail_row = jnp.exp(total - cum_row)

    def per_head(fn):
        return jnp.stack([fn(h) for h in range(heads)])

    decay_mat = per_head(
        lambda h: jnp.exp(
            jnp.where(causal, cum_col[:, h : h + 1] - cum_row[h : h + 1, :], -1e30)
        )
    )
    strict_part = per_head(
        lambda h: jnp.where(
            strict, beta_col[:, h : h + 1] * gram[h // group] * decay_mat[h], 0.0
        )
    )
    inverse = unit_lower_inverse(strict_part)
    scaled = per_head(lambda h: inverse[h] * beta_row[h : h + 1, :])
    wy = mm_split(
        per_head(lambda h: scaled[h] * (exp_row[h : h + 1, :] * r_row[h // group])),
        per_head(lambda h: keys[h // group]),
    )
    tails = per_head(
        lambda h: keys_t32[h // group] * (r_row[h // group] * tail_row[h : h + 1, :])
    )
    moved = mm3(tails, wy)
    for h in range(heads):
        own_t[h] = exp_total[h : h + 1, :] * eye - moved[h]

    pl.semaphore_wait(barrier, greeted)

    def head_copy(k):
        h = (z // 2 + k) % heads
        return pltpu.make_async_remote_copy(
            src_ref=own_t.at[h],
            dst_ref=zin_t.at[z],
            send_sem=zsend_t.at[k],
            recv_sem=zrecv_t.at[z],
            device_id=(y * nz + 2 * h + core, head),
            device_id_type=MESH,
        )

    def part(p):
        return pl.ds(p * ROWS, ROWS)

    def head_part_copy(k, p):
        h = (z // 2 + k) % heads
        return pltpu.make_async_remote_copy(
            src_ref=own_s.at[h, part(p)],
            dst_ref=zin_s.at[z, part(p)],
            send_sem=zsend_s.at[p, k],
            recv_sem=zrecv_s.at[p, z],
            device_id=(y * nz + 2 * h + core, head),
            device_id_type=MESH,
        )

    def each_head_copy(act):
        for k in by_distance:
            if k:
                act(head_copy(k))
            else:

                @pl.when(jnp.logical_not(worker))
                def _():
                    act(head_copy(0))

    def each_head_part_copy(act):
        for p in range(PARTS):
            for k in by_distance:
                if k:
                    act(head_part_copy(k, p))
                else:

                    @pl.when(jnp.logical_not(worker))
                    def _():
                        act(head_part_copy(0, p))

    def keep_own(own, zin):
        @pl.when(worker)
        def _():
            zin[pl.ds(z, 1)] = own[pl.ds(z // 2, 1)]

    by_distance = sorted(range(heads), key=lambda k: -min(k, heads - k))
    each_head_copy(lambda copy: copy.start())
    keep_own(own_t, zin_t)
    loads[3].wait()
    values = jnp.stack([v_ref[:, i * D : (i + 1) * D] for i in range(heads)])
    pseudo = mm_split(scaled, values)
    gained = mm3(tails, pseudo)
    for h in range(heads):
        own_s[h] = gained[h].T
    each_head_part_copy(lambda copy: copy.start())
    keep_own(own_s, zin_s)

    loads[4].wait()
    queries = jnp.stack([q_ref[:, i * D : (i + 1) * D] for i in range(kheads)])
    scores = mm_bf16(queries, keys_t) * r_row
    exp_col = jnp.exp(cum_col)
    wy_pseudo = jnp.concatenate([wy, pseudo], axis=2)
    mixed = mm3(per_head(lambda h: scores[h // group] * decay_mat[h]), wy_pseudo)
    for h in range(heads):
        within[h] = mixed[h, :, D:]
        qmap[h] = exp_col[:, h : h + 1] * queries[h // group].astype(F32) - mixed[h, :, :D]
    for copy in loads[5:]:
        copy.wait()
    for h in range(heads):
        gate = gate_ref[:, h * D : (h + 1) * D].astype(F32)
        gating[h] = gain_ref[...] * (gate / (1.0 + jnp.exp(-gate)))

    def row_copy(dy):
        return pltpu.make_async_remote_copy(
            src_ref=total_t,
            dst_ref=yin_t.at[dy],
            send_sem=ysend_t.at[dy],
            recv_sem=yrecv_t.at[dy],
            device_id=((y + dy) * nz + z, head),
            device_id_type=MESH,
        )

    def row_part_copy(dy, p):
        return pltpu.make_async_remote_copy(
            src_ref=total_s.at[part(p)],
            dst_ref=yin_s.at[dy, part(p)],
            send_sem=ysend_s.at[p, dy],
            recv_sem=yrecv_s.at[p, dy],
            device_id=((y + dy) * nz + z, head),
            device_id_type=MESH,
        )

    far_rows = sorted(range(1, ny), key=lambda d: -min(d, ny - d))

    def each_row_t(act):
        for dy in far_rows:

            @pl.when((y > 0) & (y + dy < ny))
            def _():
                act(row_copy(dy))

    def each_row_s(act, p):
        for dy in far_rows:

            @pl.when(y + dy < ny)
            def _():
                act(row_part_copy(dy, p))

    def state_copy(dz, p):
        i = (z + dz) % nz
        return pltpu.make_async_remote_copy(
            src_ref=sout.at[i, part(p)],
            dst_ref=sin.at[z // 2, part(p)],
            send_sem=rsend.at[p, dz],
            recv_sem=rrecv.at[p, z // 2],
            device_id=(y * nz + i, head),
            device_id_type=MESH,
        )

    def arrived(dst, sem):
        pltpu.make_async_remote_copy(
            src_ref=dst,
            dst_ref=dst,
            send_sem=zsend_t.at[0],
            recv_sem=sem,
            device_id=(ctx, sibling),
            device_id_type=MESH,
        ).wait_recv()

    targets = sorted(range(nz), key=lambda d: -min(d, nz - d))

    @pl.when(worker)
    def _():
        for i in range(nz):

            @pl.when(z != i)
            def _():
                arrived(zin_t.at[i], zrecv_t.at[i])

        first = {(i, i + 1): zin_t[i] for i in range(nz)}

        def trans(low, high):
            if (low, high) not in first:
                span = 1 << ((high - low - 1).bit_length() - 1)
                middle = low + span if low % (2 * span) == 0 else high - span
                first[(low, high)] = mm3(trans(middle, high), trans(low, middle))
            return first[(low, high)]

        total_t[...] = trans(0, nz)
        each_row_t(lambda copy: copy.start())
        for i in range(1, nz):
            suffix[:, (i - 1) * D : i * D] = trans(i, nz)
        prefix_high[0] = eye.astype(BF16)
        prefix_low[0] = jnp.zeros((D, D), BF16)
        for i in range(1, nz):
            prefix_high[i], prefix_low[i] = cut(trans(0, i))

        suffix_cut = cut(suffix[...])
        for p in range(PARTS):
            for i in range(nz):

                @pl.when(z != i)
                def _():
                    arrived(zin_s.at[i, part(p)], zrecv_s.at[p, i])

            before = jnp.concatenate([zin_s[i, part(p)] for i in range(nz - 1)], axis=1)
            total_s[part(p)] = zin_s[nz - 1, part(p)] + nt3(before, suffix_cut)
            each_row_s(lambda copy: copy.start(), p)

        prefix_s[0] = jnp.zeros((D, D), F32)
        states = {(i, i + 1): zin_s[i] for i in range(nz)}

        def state_of(low, high):
            if (low, high) not in states:
                span = 1 << ((high - low - 1).bit_length() - 1)
                middle = low + span if low % (2 * span) == 0 else high - span
                states[(low, high)] = nt3(
                    state_of(low, middle), cut(trans(middle, high))
                ) + state_of(middle, high)
            return states[(low, high)]

        for i in range(1, nz):
            prefix_s[i] = state_of(0, i)

        for dy in range(1, ny):

            @pl.when(dy > y)
            def _():
                yin_s[dy] = jnp.zeros((D, D), F32)

            @pl.when(dy >= y)
            def _():
                yin_t[dy] = eye

            @pl.when(dy < y)
            def _():
                arrived(yin_t.at[dy], yrecv_t.at[dy])

        paths = {(dy, dy + 1): yin_t[dy] for dy in range(1, ny - 1)}

        def path(low, high):
            if (low, high) not in paths:
                span = 1 << ((high - low - 1).bit_length() - 1)
                paths[(low, high)] = mm3(path(low, low + span), path(low + span, high))
            return paths[(low, high)]

        reach[:, :D] = eye
        for dy in range(2, ny):
            reach[:, (dy - 1) * D : dy * D] = path(1, dy)
        reach_cut = cut(reach[...])
        for p in range(PARTS):
            for dy in range(1, ny):

                @pl.when(dy <= y)
                def _():
                    arrived(yin_s.at[dy, part(p)], yrecv_s.at[p, dy])

            rows_in = jnp.concatenate([yin_s[dy, part(p)] for dy in range(1, ny)], axis=1)
            state = nt3(rows_in, reach_cut)
            for dz in targets:
                i = (z + dz) % nz
                one = pl.ds(i, 1)
                result = (
                    nt3(state, (prefix_high[one][0], prefix_low[one][0]))
                    + prefix_s[one, part(p)][0]
                )
                if dz:
                    sout[one, part(p)] = result[None]
                    state_copy(dz, p).start()
                else:
                    sin[pl.ds(z // 2, 1), part(p)] = result[None]

    for h in range(heads):

        @pl.when(jnp.logical_not(worker) | (z // 2 != h))
        def _():
            for p in range(PARTS):
                arrived(sin.at[h, part(p)], rrecv.at[p, h])

    core_out = within[...] + nt3(qmap[...], cut(sin[...]))
    scale = lax.rsqrt(jnp.mean(core_out * core_out, axis=2, keepdims=True) + 1e-06)
    for h in range(heads):
        gated_ref[:, h * D : (h + 1) * D] = (core_out[h] * scale[h] * gating[h]).astype(BF16)

    gated = gated_ref[...]

    def columns(chip, which):
        start = pl.multiple_of((chip * 2 + which) * width, width)
        return mm_bf16(gated, weight_ref[:, pl.ds(start, width)])

    def pair_copy(step):
        return pltpu.make_async_remote_copy(
            src_ref=pair_out.at[step],
            dst_ref=pair_in.at[step],
            send_sem=psend.at[step],
            recv_sem=precv.at[step],
            device_id=(ctx, sibling),
            device_id_type=MESH,
        )

    def chip_copy(step):
        return pltpu.make_async_remote_copy(
            src_ref=mine.at[step],
            dst_ref=chip_in.at[step],
            send_sem=csend.at[step],
            recv_sem=crecv.at[step],
            device_id=(ctx, ((x + step) % chips) * 2 + core),
            device_id_type=MESH,
        )

    order = sorted(range(chips), key=lambda s: -min(s, chips - s))
    for step in order:
        pair_out[step] = columns((x + step) % chips, 1 - core)
        pair_copy(step).start()
    for step in order:
        mine[step] = columns((x + step) % chips, core)
    for step in order:
        pair_copy(step).wait_recv()
        mine[step] = mine[step] + pair_in[step]
        if step:
            chip_copy(step).start()
    each_head_copy(lambda copy: copy.wait_send())
    each_head_part_copy(lambda copy: copy.wait_send())

    @pl.when(worker)
    def _():
        each_row_t(lambda copy: copy.wait_send())
        for p in range(PARTS):
            each_row_s(lambda copy: copy.wait_send(), p)
            for dz in targets:
                if dz:
                    state_copy(dz, p).wait_send()

    for step in order:
        pair_copy(step).wait_send()

    summed = mine[0]
    for step in order[1:-1] + order[:-1][:1]:
        chip_copy(step).wait_recv()
        summed = summed + chip_in[step]
    out_ref[...] = summed.astype(BF16)

    for step in order:
        if step:
            chip_copy(step).wait_send()


def per_device(
    queries, key_rows, value_rows, beta_logit, log_decay, out_gate, norm_gain, out_weight
):
    heads = value_rows.shape[1] // D
    tokens = value_rows.shape[0]
    nz = 2 * heads
    ny = lax.axis_size("ctx") // nz
    n = lax.axis_size("head")
    width = out_weight.shape[1] // n
    vmem = pltpu.VMEM
    dma = pltpu.SemaphoreType.DMA
    args = (
        queries,
        key_rows,
        value_rows,
        beta_logit.T,
        log_decay.T,
        out_gate,
        norm_gain[None],
        out_weight,
    )
    return pl.pallas_call(
        functools.partial(kernel, ny, nz, n),
        out_shape=vmem((tokens, width), BF16),
        in_specs=[pl.BlockSpec(memory_space=pltpu.HBM)] * len(args),
        out_specs=pl.BlockSpec(memory_space=vmem),
        scratch_shapes=[vmem(a.shape, a.dtype) for a in args]
        + [
            vmem((heads, D, D), F32),
            vmem((heads, D, D), F32),
            vmem((nz, D, D), F32),
            vmem((nz, D, D), F32),
            vmem((ny, D, D), F32),
            vmem((ny, D, D), F32),
            vmem((D, D), F32),
            vmem((D, D), F32),
            vmem((nz, D, D), BF16),
            vmem((nz, D, D), BF16),
            vmem((nz, D, D), F32),
            vmem((D, (nz - 1) * D), F32),
            vmem((D, (ny - 1) * D), F32),
            vmem((nz, D, D), F32),
            vmem((heads, D, D), F32),
            vmem((heads, D, D), F32),
            vmem((heads, D, D), F32),
            vmem((heads, D, D), F32),
            vmem((tokens, heads * D), BF16),
            vmem((n // 2, tokens, width), F32),
            vmem((n // 2, tokens, width), F32),
            vmem((n // 2, tokens, width), F32),
            vmem((n // 2, tokens, width), F32),
            dma((len(args),)),
            dma((heads,)),
            dma((PARTS, heads)),
            dma((nz,)),
            dma((PARTS, nz)),
            dma((ny,)),
            dma((PARTS, ny)),
            dma((ny,)),
            dma((PARTS, ny)),
            dma((PARTS, nz)),
            dma((PARTS, heads)),
            dma((n // 2,)),
            dma((n // 2,)),
            dma((n // 2,)),
            dma((n // 2,)),
        ],
        compiler_params=pltpu.CompilerParams(
            collective_id=0, has_side_effects=True, vmem_limit_bytes=56 * 2**20
        ),
        name="delta_layer",
    )(*args)


def solution(mesh):
    return jax.shard_map(
        per_device,
        mesh=mesh,
        in_specs=(
            P("ctx", "head"),
            P("ctx", "head"),
            P("ctx", "head"),
            P("ctx", "head"),
            P("ctx", "head"),
            P("ctx", "head"),
            P(),
            P("head", None),
        ),
        out_specs=P("ctx", "head"),
        check_vma=False,
    )
```

```python
import functools

import jax
import jax.numpy as jnp
from jax import lax
from jax.experimental import pallas as pl
from jax.experimental.pallas import tpu as pltpu
from jax.sharding import PartitionSpec as P

MESH = pl.DeviceIdType.MESH
F32 = jnp.float32
BF16 = jnp.bfloat16
D = 128
PARTS = 2
ROWS = D // PARTS


def mm(a, b):
    batch = tuple(range(a.ndim - 2))
    dims = (((a.ndim - 1,), (b.ndim - 2,)), (batch, batch))
    return lax.dot_general(a, b, dims, precision=lax.Precision.HIGHEST, preferred_element_type=F32)


def mm_bf16(a, b):
    batch = tuple(range(a.ndim - 2))
    dims = (((a.ndim - 1,), (b.ndim - 2,)), (batch, batch))
    return lax.dot_general(a, b, dims, preferred_element_type=F32)


def mm_split(a, b):
    high = a.astype(BF16)
    low = (a - high.astype(F32)).astype(BF16)
    return mm_bf16(high, b) + mm_bf16(low, b)


def cut(a):
    high = a.astype(BF16)
    return high, (a - high.astype(F32)).astype(BF16)


def mm3(a, b):
    a_high, a_low = cut(a)
    b_high, b_low = cut(b)
    return mm_bf16(a_high, b_high) + (mm_bf16(a_high, b_low) + mm_bf16(a_low, b_high))


def nt3(a, b_cut):
    batch = tuple(range(a.ndim - 2))
    dims = (((a.ndim - 1,), (a.ndim - 1,)), (batch, batch))

    def dot(left, right):
        return lax.dot_general(left, right, dims, preferred_element_type=F32)

    a_high, a_low = cut(a)
    b_high, b_low = b_cut
    return dot(a_high, b_high) + (dot(a_high, b_low) + dot(a_low, b_high))


def nt(a, b):
    return lax.dot_general(
        a, b, (((1,), (1,)), ((), ())), precision=lax.Precision.HIGHEST, preferred_element_type=F32
    )


def iotas(n):
    return (
        lax.broadcasted_iota(jnp.int32, (n, n), 0),
        lax.broadcasted_iota(jnp.int32, (n, n), 1),
    )


def unit_lower_inverse(strict_part):
    row, col = iotas(D)
    eye = jnp.where(row == col, 1.0, 0.0).astype(F32)

    def off(half):
        shift = half.bit_length() - 1
        rb, cb = row >> shift, col >> shift
        mask = ((rb ^ cb) == 1) & (rb > cb)
        return jnp.where(mask[None], strict_part, 0.0)

    inverse = eye[None] - off(1)
    half = 2
    while half < D:
        inverse = inverse - mm3(inverse, mm3(off(half), inverse))
        half *= 2
    return inverse


def kernel(
    ny,
    nz,
    n,
    q_hbm,
    k_hbm,
    v_hbm,
    beta_hbm,
    decay_hbm,
    gate_hbm,
    gain_hbm,
    weight_hbm,
    out_ref,
    q_ref,
    k_ref,
    v_ref,
    beta_ref,
    decay_ref,
    gate_ref,
    gain_ref,
    weight_ref,
    own_t,
    own_s,
    zin_t,
    zin_s,
    yin_t,
    yin_s,
    total_t,
    total_s,
    prefix_high,
    prefix_low,
    prefix_s,
    suffix,
    reach,
    sout,
    sin,
    within,
    qmap,
    gating,
    gated_ref,
    pair_out,
    pair_in,
    mine,
    chip_in,
    load,
    zsend_t,
    zsend_s,
    zrecv_t,
    zrecv_s,
    ysend_t,
    ysend_s,
    yrecv_t,
    yrecv_s,
    rsend,
    rrecv,
    psend,
    precv,
    csend,
    crecv,
):
    heads = v_ref.shape[1] // D
    kheads = k_ref.shape[1] // D
    group = heads // kheads
    chips = n // 2
    width = out_ref.shape[1]
    ctx, head = lax.axis_index("ctx"), lax.axis_index("head")
    y, z = ctx // nz, ctx % nz
    x, core = head // 2, head % 2
    sibling = x * 2 + 1 - core
    worker = z % 2 == core

    loads = [
        pltpu.make_async_copy(src, dst, load.at[i])
        for i, (src, dst) in enumerate(
            [
                (k_hbm, k_ref),
                (decay_hbm, decay_ref),
                (beta_hbm, beta_ref),
                (v_hbm, v_ref),
                (q_hbm, q_ref),
                (gate_hbm, gate_ref),
                (gain_hbm, gain_ref),
                (weight_hbm, weight_ref),
            ]
        )
    ]
    for copy in loads[:5]:
        copy.start()

    barrier = pltpu.get_barrier_semaphore()

    def greet(where):
        pl.semaphore_signal(barrier, inc=1, device_id=where, device_id_type=MESH)

    for dz in range(1, nz):
        greet((y * nz + (z + dz) % nz, head))
    for dy in range(1, ny):
        greet((((y + dy) % ny) * nz + z, head))
    greet((ctx, sibling))
    for dx in range(1, chips):
        greet((ctx, ((x + dx) % chips) * 2 + core))
    greeted = nz - 1 + ny - 1 + chips

    for copy in loads[:3]:
        copy.wait()
    for copy in loads[5:]:
        copy.start()

    row, col = iotas(D)
    causal, strict = row >= col, row > col
    eye = jnp.where(row == col, 1.0, 0.0).astype(F32)
    tri = jnp.where(causal, 1.0, 0.0).astype(F32)
    keys = jnp.stack([k_ref[:, i * D : (i + 1) * D] for i in range(kheads)])
    keys32 = keys.astype(F32)
    keys_t32 = jnp.stack([keys32[i].T for i in range(kheads)])
    keys_t = keys_t32.astype(BF16)
    r_col = lax.rsqrt(jnp.sum(keys32 * keys32, axis=2, keepdims=True) + 1e-06)
    r_row = lax.rsqrt(jnp.sum(keys_t32 * keys_t32, axis=1, keepdims=True) + 1e-06)
    gram = mm_bf16(keys, keys_t) * (r_col * r_row)

    beta_row = jax.nn.sigmoid(beta_ref[...])
    decay_row = decay_ref[...]
    cum_row = nt(decay_row, tri)
    cum_col = nt(tri, decay_row)
    beta_col = nt(eye, beta_row)
    exp_row = jnp.exp(cum_row)
    total = cum_row[:, D - 1 : D]
    exp_total = jnp.exp(total)
    tail_row = jnp.exp(total - cum_row)

    def per_head(fn):
        return jnp.stack([fn(h) for h in range(heads)])

    decay_mat = per_head(
        lambda h: jnp.exp(
            jnp.where(causal, cum_col[:, h : h + 1] - cum_row[h : h + 1, :], -1e30)
        )
    )
    strict_part = per_head(
        lambda h: jnp.where(
            strict, beta_col[:, h : h + 1] * gram[h // group] * decay_mat[h], 0.0
        )
    )
    inverse = unit_lower_inverse(strict_part)
    scaled = per_head(lambda h: inverse[h] * beta_row[h : h + 1, :])
    wy = mm_split(
        per_head(lambda h: scaled[h] * (exp_row[h : h + 1, :] * r_row[h // group])),
        per_head(lambda h: keys[h // group]),
    )
    tails = per_head(
        lambda h: keys_t32[h // group] * (r_row[h // group] * tail_row[h : h + 1, :])
    )
    moved = mm3(tails, wy)
    for h in range(heads):
        own_t[h] = exp_total[h : h + 1, :] * eye - moved[h]

    pl.semaphore_wait(barrier, greeted)

    def head_copy(k):
        h = (z // 2 + k * (1 - 2 * (z % 2)) + heads) % heads
        return pltpu.make_async_remote_copy(
            src_ref=own_t.at[h],
            dst_ref=zin_t.at[z],
            send_sem=zsend_t.at[k],
            recv_sem=zrecv_t.at[z],
            device_id=(y * nz + 2 * h + core, head),
            device_id_type=MESH,
        )

    def part(p):
        return pl.ds(p * ROWS, ROWS)

    def head_part_copy(k, p):
        h = (z // 2 + k * (1 - 2 * (z % 2)) + heads) % heads
        return pltpu.make_async_remote_copy(
            src_ref=own_s.at[h, part(p)],
            dst_ref=zin_s.at[z, part(p)],
            send_sem=zsend_s.at[p, k],
            recv_sem=zrecv_s.at[p, z],
            device_id=(y * nz + 2 * h + core, head),
            device_id_type=MESH,
        )

    def each_head_copy(act):
        for k in by_distance:
            if k:
                act(head_copy(k))
            else:

                @pl.when(jnp.logical_not(worker))
                def _():
                    act(head_copy(0))

    def each_head_part_copy(act):
        for p in range(PARTS):
            for k in by_distance:
                if k:
                    act(head_part_copy(k, p))
                else:

                    @pl.when(jnp.logical_not(worker))
                    def _():
                        act(head_part_copy(0, p))

    def keep_own(own, zin):
        @pl.when(worker)
        def _():
            zin[pl.ds(z, 1)] = own[pl.ds(z // 2, 1)]

    by_distance = sorted(range(heads), key=lambda k: -min(k, heads - k))
    each_head_copy(lambda copy: copy.start())
    keep_own(own_t, zin_t)
    loads[3].wait()
    values = jnp.stack([v_ref[:, i * D : (i + 1) * D] for i in range(heads)])
    pseudo = mm_split(scaled, values)
    gained = mm3(tails, pseudo)
    for h in range(heads):
        own_s[h] = gained[h].T
    each_head_part_copy(lambda copy: copy.start())
    keep_own(own_s, zin_s)

    loads[4].wait()
    queries = jnp.stack([q_ref[:, i * D : (i + 1) * D] for i in range(kheads)])
    scores = mm_bf16(queries, keys_t) * r_row
    exp_col = jnp.exp(cum_col)
    wy_pseudo = jnp.concatenate([wy, pseudo], axis=2)
    mixed = mm3(per_head(lambda h: scores[h // group] * decay_mat[h]), wy_pseudo)
    for h in range(heads):
        within[h] = mixed[h, :, D:]
        qmap[h] = exp_col[:, h : h + 1] * queries[h // group].astype(F32) - mixed[h, :, :D]
    for copy in loads[5:]:
        copy.wait()
    for h in range(heads):
        gate = gate_ref[:, h * D : (h + 1) * D].astype(F32)
        gating[h] = gain_ref[...] * (gate / (1.0 + jnp.exp(-gate)))

    def row_copy(dy):
        return pltpu.make_async_remote_copy(
            src_ref=total_t,
            dst_ref=yin_t.at[dy],
            send_sem=ysend_t.at[dy],
            recv_sem=yrecv_t.at[dy],
            device_id=((y + dy) * nz + z, head),
            device_id_type=MESH,
        )

    def row_part_copy(dy, p):
        return pltpu.make_async_remote_copy(
            src_ref=total_s.at[part(p)],
            dst_ref=yin_s.at[dy, part(p)],
            send_sem=ysend_s.at[p, dy],
            recv_sem=yrecv_s.at[p, dy],
            device_id=((y + dy) * nz + z, head),
            device_id_type=MESH,
        )

    far_rows = sorted(range(1, ny), key=lambda d: -min(d, ny - d))

    def each_row_t(act):
        for dy in far_rows:

            @pl.when((y > 0) & (y + dy < ny))
            def _():
                act(row_copy(dy))

    def each_row_s(act, p):
        for dy in far_rows:

            @pl.when(y + dy < ny)
            def _():
                act(row_part_copy(dy, p))

    def state_copy(dz, p):
        i = (z + dz) % nz
        return pltpu.make_async_remote_copy(
            src_ref=sout.at[i, part(p)],
            dst_ref=sin.at[z // 2, part(p)],
            send_sem=rsend.at[p, dz],
            recv_sem=rrecv.at[p, z // 2],
            device_id=(y * nz + i, head),
            device_id_type=MESH,
        )

    def arrived(dst, sem):
        pltpu.make_async_remote_copy(
            src_ref=dst,
            dst_ref=dst,
            send_sem=zsend_t.at[0],
            recv_sem=sem,
            device_id=(ctx, sibling),
            device_id_type=MESH,
        ).wait_recv()

    targets = sorted(range(nz), key=lambda d: -min(d, nz - d))

    @pl.when(worker)
    def _():
        for i in range(nz):

            @pl.when(z != i)
            def _():
                arrived(zin_t.at[i], zrecv_t.at[i])

        first = {(i, i + 1): zin_t[i] for i in range(nz)}

        def trans(low, high):
            if (low, high) not in first:
                span = 1 << ((high - low - 1).bit_length() - 1)
                middle = low + span if low % (2 * span) == 0 else high - span
                first[(low, high)] = mm3(trans(middle, high), trans(low, middle))
            return first[(low, high)]

        total_t[...] = trans(0, nz)
        each_row_t(lambda copy: copy.start())
        for i in range(1, nz):
            suffix[:, (i - 1) * D : i * D] = trans(i, nz)
        prefix_high[0] = eye.astype(BF16)
        prefix_low[0] = jnp.zeros((D, D), BF16)
        for i in range(1, nz):
            prefix_high[i], prefix_low[i] = cut(trans(0, i))

        suffix_cut = cut(suffix[...])
        for p in range(PARTS):
            for i in range(nz):

                @pl.when(z != i)
                def _():
                    arrived(zin_s.at[i, part(p)], zrecv_s.at[p, i])

            before = jnp.concatenate([zin_s[i, part(p)] for i in range(nz - 1)], axis=1)
            total_s[part(p)] = zin_s[nz - 1, part(p)] + nt3(before, suffix_cut)
            each_row_s(lambda copy: copy.start(), p)

        prefix_s[0] = jnp.zeros((D, D), F32)
        states = {(i, i + 1): zin_s[i] for i in range(nz)}

        def state_of(low, high):
            if (low, high) not in states:
                span = 1 << ((high - low - 1).bit_length() - 1)
                middle = low + span if low % (2 * span) == 0 else high - span
                states[(low, high)] = nt3(
                    state_of(low, middle), cut(trans(middle, high))
                ) + state_of(middle, high)
            return states[(low, high)]

        for i in range(1, nz):
            prefix_s[i] = state_of(0, i)

        for dy in range(1, ny):

            @pl.when(dy > y)
            def _():
                yin_s[dy] = jnp.zeros((D, D), F32)

            @pl.when(dy >= y)
            def _():
                yin_t[dy] = eye

            @pl.when(dy < y)
            def _():
                arrived(yin_t.at[dy], yrecv_t.at[dy])

        paths = {(dy, dy + 1): yin_t[dy] for dy in range(1, ny - 1)}

        def path(low, high):
            if (low, high) not in paths:
                span = 1 << ((high - low - 1).bit_length() - 1)
                paths[(low, high)] = mm3(path(low, low + span), path(low + span, high))
            return paths[(low, high)]

        reach[:, :D] = eye
        for dy in range(2, ny):
            reach[:, (dy - 1) * D : dy * D] = path(1, dy)
        reach_cut = cut(reach[...])
        for p in range(PARTS):
            for dy in range(1, ny):

                @pl.when(dy <= y)
                def _():
                    arrived(yin_s.at[dy, part(p)], yrecv_s.at[p, dy])

            rows_in = jnp.concatenate([yin_s[dy, part(p)] for dy in range(1, ny)], axis=1)
            state = nt3(rows_in, reach_cut)
            for dz in targets:
                i = (z + dz) % nz
                one = pl.ds(i, 1)
                result = (
                    nt3(state, (prefix_high[one][0], prefix_low[one][0]))
                    + prefix_s[one, part(p)][0]
                )
                if dz:
                    sout[one, part(p)] = result[None]
                    state_copy(dz, p).start()
                else:
                    sin[pl.ds(z // 2, 1), part(p)] = result[None]

    pieces = []
    for p in range(PARTS):
        for h in range(heads):

            @pl.when(jnp.logical_not(worker) | (z // 2 != h))
            def _():
                arrived(sin.at[h, part(p)], rrecv.at[p, h])

        pieces.append(nt3(qmap[...], cut(sin[:, part(p)])))

    core_out = within[...] + jnp.concatenate(pieces, axis=2)
    scale = lax.rsqrt(jnp.mean(core_out * core_out, axis=2, keepdims=True) + 1e-06)
    for h in range(heads):
        gated_ref[:, h * D : (h + 1) * D] = (core_out[h] * scale[h] * gating[h]).astype(BF16)

    gated = gated_ref[...]

    def columns(chip, which):
        start = pl.multiple_of((chip * 2 + which) * width, width)
        return mm_bf16(gated, weight_ref[:, pl.ds(start, width)])

    def pair_copy(step):
        return pltpu.make_async_remote_copy(
            src_ref=pair_out.at[step],
            dst_ref=pair_in.at[step],
            send_sem=psend.at[step],
            recv_sem=precv.at[step],
            device_id=(ctx, sibling),
            device_id_type=MESH,
        )

    def chip_copy(step):
        return pltpu.make_async_remote_copy(
            src_ref=mine.at[step],
            dst_ref=chip_in.at[step],
            send_sem=csend.at[step],
            recv_sem=crecv.at[step],
            device_id=(ctx, ((x + step) % chips) * 2 + core),
            device_id_type=MESH,
        )

    order = sorted(range(chips), key=lambda s: -min(s, chips - s))
    for step in order:
        pair_out[step] = columns((x + step) % chips, 1 - core)
        pair_copy(step).start()
    for step in order:
        mine[step] = columns((x + step) % chips, core)
    for step in order:
        pair_copy(step).wait_recv()
        mine[step] = mine[step] + pair_in[step]
        if step:
            chip_copy(step).start()
    each_head_copy(lambda copy: copy.wait_send())
    each_head_part_copy(lambda copy: copy.wait_send())

    @pl.when(worker)
    def _():
        each_row_t(lambda copy: copy.wait_send())
        for p in range(PARTS):
            each_row_s(lambda copy: copy.wait_send(), p)
            for dz in targets:
                if dz:
                    state_copy(dz, p).wait_send()

    for step in order:
        pair_copy(step).wait_send()

    summed = mine[0]
    for step in order[1:-1] + order[:-1][:1]:
        chip_copy(step).wait_recv()
        summed = summed + chip_in[step]
    out_ref[...] = summed.astype(BF16)

    for step in order:
        if step:
            chip_copy(step).wait_send()


def per_device(
    queries, key_rows, value_rows, beta_logit, log_decay, out_gate, norm_gain, out_weight
):
    heads = value_rows.shape[1] // D
    tokens = value_rows.shape[0]
    nz = 2 * heads
    ny = lax.axis_size("ctx") // nz
    n = lax.axis_size("head")
    width = out_weight.shape[1] // n
    vmem = pltpu.VMEM
    dma = pltpu.SemaphoreType.DMA
    args = (
        queries,
        key_rows,
        value_rows,
        beta_logit.T,
        log_decay.T,
        out_gate,
        norm_gain[None],
        out_weight,
    )
    return pl.pallas_call(
        functools.partial(kernel, ny, nz, n),
        out_shape=vmem((tokens, width), BF16),
        in_specs=[pl.BlockSpec(memory_space=pltpu.HBM)] * len(args),
        out_specs=pl.BlockSpec(memory_space=vmem),
        scratch_shapes=[vmem(a.shape, a.dtype) for a in args]
        + [
            vmem((heads, D, D), F32),
            vmem((heads, D, D), F32),
            vmem((nz, D, D), F32),
            vmem((nz, D, D), F32),
            vmem((ny, D, D), F32),
            vmem((ny, D, D), F32),
            vmem((D, D), F32),
            vmem((D, D), F32),
            vmem((nz, D, D), BF16),
            vmem((nz, D, D), BF16),
            vmem((nz, D, D), F32),
            vmem((D, (nz - 1) * D), F32),
            vmem((D, (ny - 1) * D), F32),
            vmem((nz, D, D), F32),
            vmem((heads, D, D), F32),
            vmem((heads, D, D), F32),
            vmem((heads, D, D), F32),
            vmem((heads, D, D), F32),
            vmem((tokens, heads * D), BF16),
            vmem((n // 2, tokens, width), F32),
            vmem((n // 2, tokens, width), F32),
            vmem((n // 2, tokens, width), F32),
            vmem((n // 2, tokens, width), F32),
            dma((len(args),)),
            dma((heads,)),
            dma((PARTS, heads)),
            dma((nz,)),
            dma((PARTS, nz)),
            dma((ny,)),
            dma((PARTS, ny)),
            dma((ny,)),
            dma((PARTS, ny)),
            dma((PARTS, nz)),
            dma((PARTS, heads)),
            dma((n // 2,)),
            dma((n // 2,)),
            dma((n // 2,)),
            dma((n // 2,)),
        ],
        compiler_params=pltpu.CompilerParams(
            collective_id=0, has_side_effects=True, vmem_limit_bytes=56 * 2**20
        ),
        name="delta_layer",
    )(*args)


def solution(mesh):
    return jax.shard_map(
        per_device,
        mesh=mesh,
        in_specs=(
            P("ctx", "head"),
            P("ctx", "head"),
            P("ctx", "head"),
            P("ctx", "head"),
            P("ctx", "head"),
            P("ctx", "head"),
            P(),
            P("head", None),
        ),
        out_specs=P("ctx", "head"),
        check_vma=False,
    )
```

```python
import functools

import jax
import jax.numpy as jnp
from jax import lax
from jax.experimental import pallas as pl
from jax.experimental.pallas import tpu as pltpu
from jax.sharding import PartitionSpec as P

MESH = pl.DeviceIdType.MESH
F32 = jnp.float32
BF16 = jnp.bfloat16
D = 128
PARTS = 2
ROWS = D // PARTS


def mm(a, b):
    batch = tuple(range(a.ndim - 2))
    dims = (((a.ndim - 1,), (b.ndim - 2,)), (batch, batch))
    return lax.dot_general(a, b, dims, precision=lax.Precision.HIGHEST, preferred_element_type=F32)


def mm_bf16(a, b):
    batch = tuple(range(a.ndim - 2))
    dims = (((a.ndim - 1,), (b.ndim - 2,)), (batch, batch))
    return lax.dot_general(a, b, dims, preferred_element_type=F32)


def mm_split(a, b):
    high = a.astype(BF16)
    low = (a - high.astype(F32)).astype(BF16)
    return mm_bf16(high, b) + mm_bf16(low, b)


def cut(a):
    high = a.astype(BF16)
    return high, (a - high.astype(F32)).astype(BF16)


def mm3(a, b):
    a_high, a_low = cut(a)
    b_high, b_low = cut(b)
    return mm_bf16(a_high, b_high) + (mm_bf16(a_high, b_low) + mm_bf16(a_low, b_high))


def nt3(a, b_cut):
    batch = tuple(range(a.ndim - 2))
    dims = (((a.ndim - 1,), (a.ndim - 1,)), (batch, batch))

    def dot(left, right):
        return lax.dot_general(left, right, dims, preferred_element_type=F32)

    a_high, a_low = cut(a)
    b_high, b_low = b_cut
    return dot(a_high, b_high) + (dot(a_high, b_low) + dot(a_low, b_high))


def nt(a, b):
    return lax.dot_general(
        a, b, (((1,), (1,)), ((), ())), precision=lax.Precision.HIGHEST, preferred_element_type=F32
    )


def iotas(n):
    return (
        lax.broadcasted_iota(jnp.int32, (n, n), 0),
        lax.broadcasted_iota(jnp.int32, (n, n), 1),
    )


def unit_lower_inverse(strict_part):
    row, col = iotas(D)
    eye = jnp.where(row == col, 1.0, 0.0).astype(F32)

    def off(half):
        shift = half.bit_length() - 1
        rb, cb = row >> shift, col >> shift
        mask = ((rb ^ cb) == 1) & (rb > cb)
        return jnp.where(mask[None], strict_part, 0.0)

    inverse = eye[None] - off(1)
    half = 2
    while half < D:
        inverse = inverse - mm3(inverse, mm3(off(half), inverse))
        half *= 2
    return inverse


def kernel(
    ny,
    nz,
    n,
    q_hbm,
    k_hbm,
    v_hbm,
    beta_hbm,
    decay_hbm,
    gate_hbm,
    gain_hbm,
    weight_hbm,
    out_ref,
    q_ref,
    k_ref,
    v_ref,
    beta_ref,
    decay_ref,
    gate_ref,
    gain_ref,
    weight_ref,
    own_t,
    own_s,
    zin_t,
    zin_s,
    yin_t,
    yin_s,
    total_t,
    total_s,
    prefix_high,
    prefix_low,
    prefix_s,
    suffix,
    reach,
    sout,
    sin,
    within,
    qmap,
    gating,
    gated_ref,
    pair_out,
    pair_in,
    mine,
    chip_in,
    load,
    zsend_t,
    zsend_s,
    zrecv_t,
    zrecv_s,
    ysend_t,
    ysend_s,
    yrecv_t,
    yrecv_s,
    rsend,
    rrecv,
    psend,
    precv,
    csend,
    crecv,
):
    heads = v_ref.shape[1] // D
    kheads = k_ref.shape[1] // D
    group = heads // kheads
    chips = n // 2
    width = out_ref.shape[1]
    ctx, head = lax.axis_index("ctx"), lax.axis_index("head")
    y, z = ctx // nz, ctx % nz
    x, core = head // 2, head % 2
    sibling = x * 2 + 1 - core
    worker = z % 2 == core

    loads = [
        pltpu.make_async_copy(src, dst, load.at[i])
        for i, (src, dst) in enumerate(
            [
                (k_hbm, k_ref),
                (decay_hbm, decay_ref),
                (beta_hbm, beta_ref),
                (v_hbm, v_ref),
                (q_hbm, q_ref),
                (gate_hbm, gate_ref),
                (gain_hbm, gain_ref),
                (weight_hbm, weight_ref),
            ]
        )
    ]
    for copy in loads:
        copy.start()

    barrier = pltpu.get_barrier_semaphore()

    def greet(where):
        pl.semaphore_signal(barrier, inc=1, device_id=where, device_id_type=MESH)

    for dz in range(1, nz):
        greet((y * nz + (z + dz) % nz, head))
    for dy in range(1, ny):
        greet((((y + dy) % ny) * nz + z, head))
    greet((ctx, sibling))
    for dx in range(1, chips):
        greet((ctx, ((x + dx) % chips) * 2 + core))
    greeted = nz - 1 + ny - 1 + chips

    for copy in loads[:3]:
        copy.wait()

    row, col = iotas(D)
    causal, strict = row >= col, row > col
    eye = jnp.where(row == col, 1.0, 0.0).astype(F32)
    tri = jnp.where(causal, 1.0, 0.0).astype(F32)
    keys = jnp.stack([k_ref[:, i * D : (i + 1) * D] for i in range(kheads)])
    keys32 = keys.astype(F32)
    keys_t32 = jnp.stack([keys32[i].T for i in range(kheads)])
    keys_t = keys_t32.astype(BF16)
    r_col = lax.rsqrt(jnp.sum(keys32 * keys32, axis=2, keepdims=True) + 1e-06)
    r_row = lax.rsqrt(jnp.sum(keys_t32 * keys_t32, axis=1, keepdims=True) + 1e-06)
    gram = mm_bf16(keys, keys_t) * (r_col * r_row)

    beta_row = jax.nn.sigmoid(beta_ref[...])
    decay_row = decay_ref[...]
    cum_row = nt(decay_row, tri)
    cum_col = nt(tri, decay_row)
    beta_col = nt(eye, beta_row)
    exp_row = jnp.exp(cum_row)
    total = cum_row[:, D - 1 : D]
    exp_total = jnp.exp(total)
    tail_row = jnp.exp(total - cum_row)

    def per_head(fn):
        return jnp.stack([fn(h) for h in range(heads)])

    decay_mat = per_head(
        lambda h: jnp.exp(
            jnp.where(causal, cum_col[:, h : h + 1] - cum_row[h : h + 1, :], -1e30)
        )
    )
    strict_part = per_head(
        lambda h: jnp.where(
            strict, beta_col[:, h : h + 1] * gram[h // group] * decay_mat[h], 0.0
        )
    )
    inverse = unit_lower_inverse(strict_part)
    scaled = per_head(lambda h: inverse[h] * beta_row[h : h + 1, :])
    wy = mm_split(
        per_head(lambda h: scaled[h] * (exp_row[h : h + 1, :] * r_row[h // group])),
        per_head(lambda h: keys[h // group]),
    )
    tails = per_head(
        lambda h: keys_t32[h // group] * (r_row[h // group] * tail_row[h : h + 1, :])
    )
    moved = mm3(tails, wy)
    for h in range(heads):
        own_t[h] = exp_total[h : h + 1, :] * eye - moved[h]

    pl.semaphore_wait(barrier, greeted)

    def head_copy(k):
        h = (z // 2 + k) % heads
        return pltpu.make_async_remote_copy(
            src_ref=own_t.at[h],
            dst_ref=zin_t.at[z],
            send_sem=zsend_t.at[k],
            recv_sem=zrecv_t.at[z],
            device_id=(y * nz + 2 * h + core, head),
            device_id_type=MESH,
        )

    def part(p):
        return pl.ds(p * ROWS, ROWS)

    def head_part_copy(k, p):
        h = (z // 2 + k) % heads
        return pltpu.make_async_remote_copy(
            src_ref=own_s.at[h],
            dst_ref=zin_s.at[z],
            send_sem=zsend_s.at[p, k],
            recv_sem=zrecv_s.at[p, z],
            device_id=(y * nz + 2 * h + core, head),
            device_id_type=MESH,
        )

    def each_head_copy(act):
        for k in by_distance:
            if k:
                act(head_copy(k))
            else:

                @pl.when(jnp.logical_not(worker))
                def _():
                    act(head_copy(0))

    def each_head_part_copy(act):
        for p in range(1):
            for k in by_distance:
                if k:
                    act(head_part_copy(k, p))
                else:

                    @pl.when(jnp.logical_not(worker))
                    def _():
                        act(head_part_copy(0, p))

    def keep_own(own, zin):
        @pl.when(worker)
        def _():
            zin[pl.ds(z, 1)] = own[pl.ds(z // 2, 1)]

    by_distance = sorted(range(heads), key=lambda k: -min(k, heads - k))
    each_head_copy(lambda copy: copy.start())
    keep_own(own_t, zin_t)
    loads[3].wait()
    values = jnp.stack([v_ref[:, i * D : (i + 1) * D] for i in range(heads)])
    pseudo = mm_split(scaled, values)
    gained = mm3(tails, pseudo)
    for h in range(heads):
        own_s[h] = gained[h].T
    each_head_part_copy(lambda copy: copy.start())
    keep_own(own_s, zin_s)

    loads[4].wait()
    queries = jnp.stack([q_ref[:, i * D : (i + 1) * D] for i in range(kheads)])
    scores = mm_bf16(queries, keys_t) * r_row
    exp_col = jnp.exp(cum_col)
    wy_pseudo = jnp.concatenate([wy, pseudo], axis=2)
    mixed = mm3(per_head(lambda h: scores[h // group] * decay_mat[h]), wy_pseudo)
    for h in range(heads):
        within[h] = mixed[h, :, D:]
        qmap[h] = exp_col[:, h : h + 1] * queries[h // group].astype(F32) - mixed[h, :, :D]
    for copy in loads[5:]:
        copy.wait()
    for h in range(heads):
        gate = gate_ref[:, h * D : (h + 1) * D].astype(F32)
        gating[h] = gain_ref[...] * (gate / (1.0 + jnp.exp(-gate)))

    def row_copy(dy):
        return pltpu.make_async_remote_copy(
            src_ref=total_t,
            dst_ref=yin_t.at[dy],
            send_sem=ysend_t.at[dy],
            recv_sem=yrecv_t.at[dy],
            device_id=((y + dy) * nz + z, head),
            device_id_type=MESH,
        )

    def row_part_copy(dy, p):
        return pltpu.make_async_remote_copy(
            src_ref=total_s.at[part(p)],
            dst_ref=yin_s.at[dy, part(p)],
            send_sem=ysend_s.at[p, dy],
            recv_sem=yrecv_s.at[p, dy],
            device_id=((y + dy) * nz + z, head),
            device_id_type=MESH,
        )

    far_rows = sorted(range(1, ny), key=lambda d: -min(d, ny - d))

    def each_row_t(act):
        for dy in far_rows:

            @pl.when((y > 0) & (y + dy < ny))
            def _():
                act(row_copy(dy))

    def each_row_s(act, p):
        for dy in far_rows:

            @pl.when(y + dy < ny)
            def _():
                act(row_part_copy(dy, p))

    def state_copy(dz, p):
        i = (z + dz) % nz
        return pltpu.make_async_remote_copy(
            src_ref=sout.at[i, part(p)],
            dst_ref=sin.at[z // 2, part(p)],
            send_sem=rsend.at[p, dz],
            recv_sem=rrecv.at[p, z // 2],
            device_id=(y * nz + i, head),
            device_id_type=MESH,
        )

    def arrived(dst, sem):
        pltpu.make_async_remote_copy(
            src_ref=dst,
            dst_ref=dst,
            send_sem=zsend_t.at[0],
            recv_sem=sem,
            device_id=(ctx, sibling),
            device_id_type=MESH,
        ).wait_recv()

    targets = sorted(range(nz), key=lambda d: -min(d, nz - d))

    @pl.when(worker)
    def _():
        for i in range(nz):

            @pl.when(z != i)
            def _():
                arrived(zin_t.at[i], zrecv_t.at[i])

        first = {(i, i + 1): zin_t[i] for i in range(nz)}

        def trans(low, high):
            if (low, high) not in first:
                span = 1 << ((high - low - 1).bit_length() - 1)
                middle = low + span if low % (2 * span) == 0 else high - span
                first[(low, high)] = mm3(trans(middle, high), trans(low, middle))
            return first[(low, high)]

        total_t[...] = trans(0, nz)
        each_row_t(lambda copy: copy.start())
        for i in range(1, nz):
            suffix[:, (i - 1) * D : i * D] = trans(i, nz)
        prefix_high[0] = eye.astype(BF16)
        prefix_low[0] = jnp.zeros((D, D), BF16)
        for i in range(1, nz):
            prefix_high[i], prefix_low[i] = cut(trans(0, i))

        suffix_cut = cut(suffix[...])
        for p in range(PARTS):
            for i in range(nz if p == 0 else 0):

                @pl.when(z != i)
                def _():
                    arrived(zin_s.at[i], zrecv_s.at[p, i])

            before = jnp.concatenate([zin_s[i, part(p)] for i in range(nz - 1)], axis=1)
            total_s[part(p)] = zin_s[nz - 1, part(p)] + nt3(before, suffix_cut)
            each_row_s(lambda copy: copy.start(), p)

        prefix_s[0] = jnp.zeros((D, D), F32)
        states = {(i, i + 1): zin_s[i] for i in range(nz)}

        def state_of(low, high):
            if (low, high) not in states:
                span = 1 << ((high - low - 1).bit_length() - 1)
                middle = low + span if low % (2 * span) == 0 else high - span
                states[(low, high)] = nt3(
                    state_of(low, middle), cut(trans(middle, high))
                ) + state_of(middle, high)
            return states[(low, high)]

        for i in range(1, nz):
            prefix_s[i] = state_of(0, i)

        for dy in range(1, ny):

            @pl.when(dy > y)
            def _():
                yin_s[dy] = jnp.zeros((D, D), F32)

            @pl.when(dy >= y)
            def _():
                yin_t[dy] = eye

            @pl.when(dy < y)
            def _():
                arrived(yin_t.at[dy], yrecv_t.at[dy])

        paths = {(dy, dy + 1): yin_t[dy] for dy in range(1, ny - 1)}

        def path(low, high):
            if (low, high) not in paths:
                span = 1 << ((high - low - 1).bit_length() - 1)
                paths[(low, high)] = mm3(path(low, low + span), path(low + span, high))
            return paths[(low, high)]

        reach[:, :D] = eye
        for dy in range(2, ny):
            reach[:, (dy - 1) * D : dy * D] = path(1, dy)
        reach_cut = cut(reach[...])
        for p in range(PARTS):
            for dy in range(1, ny):

                @pl.when(dy <= y)
                def _():
                    arrived(yin_s.at[dy, part(p)], yrecv_s.at[p, dy])

            rows_in = jnp.concatenate([yin_s[dy, part(p)] for dy in range(1, ny)], axis=1)
            state = nt3(rows_in, reach_cut)
            for dz in targets:
                i = (z + dz) % nz
                one = pl.ds(i, 1)
                result = (
                    nt3(state, (prefix_high[one][0], prefix_low[one][0]))
                    + prefix_s[one, part(p)][0]
                )
                if dz:
                    sout[one, part(p)] = result[None]
                    state_copy(dz, p).start()
                else:
                    sin[pl.ds(z // 2, 1), part(p)] = result[None]

    for h in range(heads):

        @pl.when(jnp.logical_not(worker) | (z // 2 != h))
        def _():
            for p in range(PARTS):
                arrived(sin.at[h, part(p)], rrecv.at[p, h])

    core_out = within[...] + nt3(qmap[...], cut(sin[...]))
    scale = lax.rsqrt(jnp.mean(core_out * core_out, axis=2, keepdims=True) + 1e-06)
    for h in range(heads):
        gated_ref[:, h * D : (h + 1) * D] = (core_out[h] * scale[h] * gating[h]).astype(BF16)

    gated = gated_ref[...]

    def columns(chip, which):
        start = pl.multiple_of((chip * 2 + which) * width, width)
        return mm_bf16(gated, weight_ref[:, pl.ds(start, width)])

    def pair_copy(step):
        return pltpu.make_async_remote_copy(
            src_ref=pair_out.at[step],
            dst_ref=pair_in.at[step],
            send_sem=psend.at[step],
            recv_sem=precv.at[step],
            device_id=(ctx, sibling),
            device_id_type=MESH,
        )

    def chip_copy(step):
        return pltpu.make_async_remote_copy(
            src_ref=mine.at[step],
            dst_ref=chip_in.at[step],
            send_sem=csend.at[step],
            recv_sem=crecv.at[step],
            device_id=(ctx, ((x + step) % chips) * 2 + core),
            device_id_type=MESH,
        )

    order = sorted(range(chips), key=lambda s: -min(s, chips - s))
    for step in order:
        pair_out[step] = columns((x + step) % chips, 1 - core)
        pair_copy(step).start()
    for step in order:
        mine[step] = columns((x + step) % chips, core)
    for step in order:
        pair_copy(step).wait_recv()
        mine[step] = mine[step] + pair_in[step]
        if step:
            chip_copy(step).start()
    each_head_copy(lambda copy: copy.wait_send())
    each_head_part_copy(lambda copy: copy.wait_send())

    @pl.when(worker)
    def _():
        each_row_t(lambda copy: copy.wait_send())
        for p in range(PARTS):
            each_row_s(lambda copy: copy.wait_send(), p)
            for dz in targets:
                if dz:
                    state_copy(dz, p).wait_send()

    for step in order:
        pair_copy(step).wait_send()

    summed = mine[0]
    for step in order[1:-1] + order[:-1][:1]:
        chip_copy(step).wait_recv()
        summed = summed + chip_in[step]
    out_ref[...] = summed.astype(BF16)

    for step in order:
        if step:
            chip_copy(step).wait_send()


def per_device(
    queries, key_rows, value_rows, beta_logit, log_decay, out_gate, norm_gain, out_weight
):
    heads = value_rows.shape[1] // D
    tokens = value_rows.shape[0]
    nz = 2 * heads
    ny = lax.axis_size("ctx") // nz
    n = lax.axis_size("head")
    width = out_weight.shape[1] // n
    vmem = pltpu.VMEM
    dma = pltpu.SemaphoreType.DMA
    args = (
        queries,
        key_rows,
        value_rows,
        beta_logit.T,
        log_decay.T,
        out_gate,
        norm_gain[None],
        out_weight,
    )
    return pl.pallas_call(
        functools.partial(kernel, ny, nz, n),
        out_shape=vmem((tokens, width), BF16),
        in_specs=[pl.BlockSpec(memory_space=pltpu.HBM)] * len(args),
        out_specs=pl.BlockSpec(memory_space=vmem),
        scratch_shapes=[vmem(a.shape, a.dtype) for a in args]
        + [
            vmem((heads, D, D), F32),
            vmem((heads, D, D), F32),
            vmem((nz, D, D), F32),
            vmem((nz, D, D), F32),
            vmem((ny, D, D), F32),
            vmem((ny, D, D), F32),
            vmem((D, D), F32),
            vmem((D, D), F32),
            vmem((nz, D, D), BF16),
            vmem((nz, D, D), BF16),
            vmem((nz, D, D), F32),
            vmem((D, (nz - 1) * D), F32),
            vmem((D, (ny - 1) * D), F32),
            vmem((nz, D, D), F32),
            vmem((heads, D, D), F32),
            vmem((heads, D, D), F32),
            vmem((heads, D, D), F32),
            vmem((heads, D, D), F32),
            vmem((tokens, heads * D), BF16),
            vmem((n // 2, tokens, width), F32),
            vmem((n // 2, tokens, width), F32),
            vmem((n // 2, tokens, width), F32),
            vmem((n // 2, tokens, width), F32),
            dma((len(args),)),
            dma((heads,)),
            dma((PARTS, heads)),
            dma((nz,)),
            dma((PARTS, nz)),
            dma((ny,)),
            dma((PARTS, ny)),
            dma((ny,)),
            dma((PARTS, ny)),
            dma((PARTS, nz)),
            dma((PARTS, heads)),
            dma((n // 2,)),
            dma((n // 2,)),
            dma((n // 2,)),
            dma((n // 2,)),
        ],
        compiler_params=pltpu.CompilerParams(
            collective_id=0, has_side_effects=True, vmem_limit_bytes=56 * 2**20
        ),
        name="delta_layer",
    )(*args)


def solution(mesh):
    return jax.shard_map(
        per_device,
        mesh=mesh,
        in_specs=(
            P("ctx", "head"),
            P("ctx", "head"),
            P("ctx", "head"),
            P("ctx", "head"),
            P("ctx", "head"),
            P("ctx", "head"),
            P(),
            P("head", None),
        ),
        out_specs=P("ctx", "head"),
        check_vma=False,
    )
```
